32 devices in a mesh: lat: 8 (over z, x), dp: 4 (over y, core).
Axes of the slice: x: 2, y: 2, z: 4, core: 2. Of those that a mesh axis runs over, the one named last changes fastest.
Arguments:
- obs_feat: float32 [4, 8192, 128], P('dp', 'lat'), may hold values from -6 to 6
- obs_row: float32 [4, 8192], P('dp', 'lat'), may hold values from 0 to 2
- obs_col: float32 [4, 8192], P('dp', 'lat'), may hold values from 0 to 128
- counts: int32 [4, 8], P('dp', 'lat'), may hold values from 1 to 1024, 4096 in all within a row
- edge_index: int32 [4, 8, 2, 128], P('dp', 'lat'), may hold values from 0 to 1023
- edge_mask: int32 [4, 8, 2, 128], P('dp', 'lat'), may hold values 0 or 1
- cotangent: bfloat16 [4, 16, 128, 512], P('dp', 'lat'), may hold values from -0.06591797 to 0.06591797
- w_first: bfloat16 [1152, 512], P('dp'), may hold values from -0.1875 to 0.1875
- w_second: bfloat16 [4608, 512], P('dp'), may hold values from -0.09375 to 0.09375
Outputs:
- encoded: bfloat16 [4, 16, 128, 512], P('dp', 'lat')
- grad_first: float32 [1152, 512], P('dp', 'lat')
- grad_second: float32 [4608, 512], P('dp', 'lat')
The draws below stay inside these ranges and needn't reach their ends.
Inputs may be any that keep to these rules, and one draw needn't show every extreme that they name: `counts`: in each forecast time some band has exactly 1024 live slots.
All inputs are finite; a program needn't handle non-finite values. No bound on the sum of `counts` or of `edge_mask` on one device may be relied on, other than what follows from the above.
Results may differ from the reference program's by a relative error of at most 0.022.
Values may be sent and summed in bfloat16 or wider, within the bound.
No kernel may reach another device: no remote copies, remote signals or barrier semaphores. Data moves between devices by JAX's collectives and lax.ppermute only.
A program may use at most 128 MiB of HBM per device.

```python
import math
import jax
import jax.numpy as jnp
import numpy as np
from jax import lax

NCH = 128
HID = 512
R = 2
W = 128
OBS_DEV = 1024
EDGE = 128
ROWS = 16
OBS_ALL = 8192
N_LAT = 8
N_DP = 4


def set_ends(array, rng, low, largest):
    dims = array.shape
    place = [jax.random.randint(jax.random.fold_in(rng, axis), (), 0, dims[axis]) for axis in range(len(dims))]
    array = array.at[tuple(place)].set(low)
    longest = dims.index(max(dims))
    place[longest] = (place[longest] + 1) % dims[longest]
    return array.at[tuple(place)].set(largest)


def level_of(rng, shape, cuts, smallest, largest):
    level, own = 1.0, jax.random.fold_in(rng, 6)
    for dim, blocks in cuts:
        steps = jnp.exp(jax.random.uniform(jax.random.fold_in(own, dim), (blocks,), jnp.float32, smallest / len(cuts), largest / len(cuts)))
        level = level * jnp.repeat(steps, shape[dim] // blocks).reshape([-1 if axis == dim else 1 for axis in range(len(shape))])
    return level


def split_up(number_of, total, reach, skew):
    portions = [(1 << 20) // math.isqrt(rank ** skew) + 1 for rank in range(2, number_of + 1)]
    surplus, given = total - reach - (number_of - 1), [1] * (number_of - 1)
    while surplus > 0:
        free = [i for i in range(number_of - 1) if given[i] < reach]
        mass, budget = sum([portions[i] for i in free]), surplus
        for i in free:
            more = min(reach - given[i], max(1, budget * portions[i] // mass), surplus)
            given[i] = given[i] + more
            surplus = surplus - more
    return np.array([reach] + given)


def uneven(key, amount, total, reach, skew):
    if amount == 2:
        one = jax.random.randint(key, (), max(1, total - reach), min(reach, total - 1) + 1)
        return jnp.stack([one, total - one])
    sizes = jnp.asarray(split_up(amount, total, reach, skew), jnp.int32)
    couples = (amount - 1) // 2
    source_of, taker = sizes[1:1 + 2 * couples:2], sizes[2:2 + 2 * couples:2]
    room = jnp.minimum(source_of - 1, reach - taker)
    moved = jax.random.randint(jax.random.fold_in(key, 1), (couples,), 0, 1 << 20) % (room + 1)
    sizes = sizes.at[1:1 + 2 * couples:2].set(source_of - moved).at[2:2 + 2 * couples:2].set(taker + moved)
    return sizes[jax.random.permutation(jax.random.fold_in(key, 2), amount)]


def normal_values(own_key, dims, scale, most, shards=(), kind=jnp.bfloat16):
    drawn = scale * jax.random.normal(own_key, dims, jnp.float32)
    if shards:
        drawn = drawn * level_of(own_key, dims, shards, -0.22, 0.18)
    return jnp.clip(drawn, -most, most).astype(kind)


def setup_inputs(seed: int = 0) -> dict:
    arg_keys = jax.random.split(jax.random.key(seed), 10)
    obs_feat = normal_values(arg_keys[0], (N_DP, OBS_ALL, NCH), 1.0, 6.0, ((0, 4), (1, 8)), jnp.float32)
    obs_row = jnp.clip(2.0 * jax.random.uniform(arg_keys[1], (N_DP, OBS_ALL), jnp.float32) ** level_of(arg_keys[1], (N_DP, OBS_ALL), ((0, 4), (1, 8)), -0.2, 0.2), 0.0, 2.0)
    obs_col = jnp.clip(128.0 * jax.random.uniform(arg_keys[2], (N_DP, OBS_ALL), jnp.float32) ** level_of(arg_keys[2], (N_DP, OBS_ALL), ((0, 4), (1, 8)), -0.2, 0.2), 0.0, 128.0)
    counts = jax.vmap(lambda own: uneven(own, N_LAT, N_LAT * OBS_DEV // 2, OBS_DEV, 2))(jax.random.split(arg_keys[3], N_DP)).reshape((N_DP, N_LAT)).astype(jnp.int32)
    edge_index = set_ends(jax.random.randint(arg_keys[4], (N_DP, N_LAT, 2, EDGE), 0, OBS_DEV), jax.random.fold_in(arg_keys[4], 1), 0, OBS_DEV - 1).astype(jnp.int32)
    edge_mask = set_ends((jax.random.randint(arg_keys[5], (N_DP, N_LAT, 2, EDGE), 0, 4) < 3).astype(jnp.int32), jax.random.fold_in(arg_keys[5], 1), 0, 1)
    cotangent = normal_values(arg_keys[6], (N_DP, ROWS, W, HID), (1.0 / (N_DP * N_LAT * R * W) ** 0.5), 0.06591797, ((0, 4), (1, 8)))
    w_first = normal_values(arg_keys[7], (9 * NCH, HID), (9 * NCH) ** -0.5, 0.1875, ((0, 4),))
    w_second = normal_values(arg_keys[8], (9 * HID, HID), (9 * HID) ** -0.5, 0.09375, ((0, 4),))
    return dict(obs_feat=obs_feat, obs_row=obs_row, obs_col=obs_col, counts=counts, edge_index=edge_index, edge_mask=edge_mask, cotangent=cotangent, w_first=w_first, w_second=w_second)


def gauss_weights(cell_rows, cell_cols, rows, cols, valid):
    drow = cell_rows[:, None] - rows[None, :]
    dcol = cell_cols[:, None] - cols[None, :]
    return valid[None, :] * jnp.exp(-0.5 * (drow * drow + dcol * dcol))

def grid_patches(grid):
    height, width = (grid.shape[0], grid.shape[1])
    padded = jnp.pad(grid, ((1, 1), (1, 1), (0, 0)))
    pieces = [padded[dy:dy + height, dx:dx + width] for dy in range(3) for dx in range(3)]
    return jnp.concatenate(pieces, axis=-1).reshape(height * width, -1)

def from_below(values):
    return jnp.concatenate([jnp.zeros_like(values[:1]), values[:-1]], 0)

def from_above(values):
    return jnp.concatenate([values[1:], jnp.zeros_like(values[:1])], 0)

def reference(obs_feat, obs_row, obs_col, counts, edge_index, edge_mask, cotangent, w_first, w_second):
    height = N_LAT * R

    def one_time(carry, inputs):
        feat, row, col, count, eidx, emask, cot = inputs
        feat = feat.reshape(N_LAT, OBS_DEV, NCH)
        band_base = (jnp.arange(N_LAT) * R).astype(jnp.float32)
        row_g = row.reshape(N_LAT, OBS_DEV) + band_base[:, None]
        col_b = col.reshape(N_LAT, OBS_DEV)
        slots = jnp.arange(OBS_DEV, dtype=jnp.int32)
        valid = (slots[None, :] < count[:, None]).astype(jnp.float32)
        e_feat = jax.vmap(lambda f, i: f[i])(feat, eidx)
        e_row = jax.vmap(lambda f, i: f[i])(row_g, eidx)
        e_col = jax.vmap(lambda f, i: f[i])(col_b, eidx)
        e_valid = emask.astype(jnp.float32) * (eidx < count[:, None, None]).astype(jnp.float32)
        all_feat = jnp.concatenate([feat, from_below(e_feat[:, 1]), from_above(e_feat[:, 0])], 1)
        all_row = jnp.concatenate([row_g, from_below(e_row[:, 1]), from_above(e_row[:, 0])], 1)
        all_col = jnp.concatenate([col_b, from_below(e_col[:, 1]), from_above(e_col[:, 0])], 1)
        all_valid = jnp.concatenate([valid, from_below(e_valid[:, 1]), from_above(e_valid[:, 0])], 1)
        cells = jnp.arange(R * W, dtype=jnp.int32)
        cell_rows = band_base[:, None] + (cells // W).astype(jnp.float32)[None, :]
        cell_cols = jnp.broadcast_to((cells % W).astype(jnp.float32)[None, :], (N_LAT, R * W))
        weights = jax.vmap(gauss_weights)(cell_rows, cell_cols, all_row, all_col, all_valid)
        numer = jnp.einsum('bpn,bnc->bpc', weights, all_feat, precision=lax.Precision.HIGHEST)
        denom = lax.optimization_barrier(jnp.sum(weights, -1))
        h0 = (numer / jnp.sqrt(1.0 + denom)[..., None]).astype(jnp.bfloat16).reshape(height, W, NCH)
        patches0 = grid_patches(h0)
        pre1 = jnp.dot(patches0, w_first, preferred_element_type=jnp.float32)
        h1 = jax.nn.silu(pre1).astype(jnp.bfloat16)
        patches1 = grid_patches(h1.reshape(height, W, HID))
        pre2 = jnp.dot(patches1, w_second, preferred_element_type=jnp.float32)
        encoded = (h1.astype(jnp.float32) + pre2).astype(jnp.bfloat16).reshape(height, W, HID)
        gpad = jnp.pad(cot, ((1, 1), (1, 1), (0, 0)))
        spread = jnp.dot(gpad.reshape(-1, HID), w_second.T, preferred_element_type=jnp.float32)
        spread = spread.reshape(height + 2, W + 2, 9, HID)
        dh1 = cot.astype(jnp.float32)
        for dy in range(3):
            for dx in range(3):
                dh1 = dh1 + spread[2 - dy:2 - dy + height, 2 - dx:2 - dx + W, dy * 3 + dx]
        sig = jax.nn.sigmoid(pre1)
        dpre1 = (dh1.reshape(-1, HID) * sig * (1.0 + pre1 * (1.0 - sig))).astype(jnp.bfloat16)
        cot_flat = cot.reshape(-1, HID)
        grad_two = jnp.dot(patches1.T, cot_flat, preferred_element_type=jnp.float32)
        grad_one = jnp.dot(patches0.T, dpre1, preferred_element_type=jnp.float32)
        return ((carry[0] + grad_one, carry[1] + grad_two), encoded)
    start = (jnp.zeros((9 * NCH, HID), jnp.float32), jnp.zeros((9 * HID, HID), jnp.float32))
    grads, encoded = lax.scan(one_time, start, (obs_feat, obs_row, obs_col, counts, edge_index, edge_mask, cotangent))
    return (encoded, grads[0], grads[1])
```

```python
import functools
import math

import jax
import jax.numpy as jnp
from jax import lax
from jax.experimental import pallas as pl
from jax.experimental.pallas import tpu as pltpu
from jax.sharding import PartitionSpec as P

BF16 = jnp.bfloat16
F32 = jnp.float32
VMEM = pl.BlockSpec(memory_space=pltpu.VMEM)
SMEM = pl.BlockSpec(memory_space=pltpu.SMEM)


def call(kernel, name, outs, scratch=(), flops=0, scalars=1):
    def run(*args):
        moved = sum(math.prod(o.shape) * o.dtype.itemsize for o in outs)
        moved += sum(a.size * a.dtype.itemsize for a in args)
        return pl.pallas_call(
            kernel,
            name=name,
            out_shape=outs,
            in_specs=[SMEM] * scalars + [VMEM] * (len(args) - scalars),
            out_specs=[VMEM] * len(outs),
            scratch_shapes=list(scratch),
            compiler_params=pltpu.CompilerParams(vmem_limit_bytes=48 * 2**20),
            cost_estimate=pl.CostEstimate(flops=flops, bytes_accessed=moved, transcendentals=0),
        )(*args)

    return run


def like(shape, dtype):
    return jax.ShapeDtypeStruct(shape, dtype)


def dot(a, b):
    return jnp.dot(a, b, preferred_element_type=F32)


def dot_nt(a, b):
    return lax.dot_general(a, b, (((1,), (1,)), ((), ())), preferred_element_type=F32)


def shifted(x, step, width):
    if isinstance(step, int) and step == 0:
        return x
    total = x.shape[0]
    wide = pltpu.roll(x.astype(F32), lax.rem(total - step, total) if not isinstance(step, int) else (total - step) % total, 0)
    place = lax.broadcasted_iota(jnp.int32, x.shape, 0) % width + step
    return jnp.where((place >= 0) & (place < width), wide, 0.0).astype(x.dtype)


def column_factor(col_ref, width):
    cells = lax.broadcasted_iota(jnp.int32, (width, col_ref.shape[1]), 0).astype(F32)
    away = cells - col_ref[...]
    return jnp.exp(-0.5 * (away * away))


def cell_weights(factor, row_ref, rows):
    parts = []
    for row in rows:
        away = row - row_ref[...]
        parts.append((factor * jnp.exp(-0.5 * (away * away))).astype(BF16))
    return jnp.concatenate(parts, axis=0)


def edge_kernel(height, width, s_ref, feat_ref, row_ref, col_ref, index_ref, mask_ref, out_ref):
    slots, channels = feat_ref.shape
    factor = column_factor(col_ref, width)
    entries = index_ref.shape[1]
    slot = lax.broadcasted_iota(jnp.int32, (slots, entries), 0)
    live = slot < s_ref[1]
    feat = feat_ref[...]
    for side in range(2):
        named = jnp.where((slot == index_ref[side : side + 1]) & live, mask_ref[side : side + 1], 0)
        times = jnp.sum(named.astype(F32), axis=1, keepdims=True)
        values = jnp.concatenate([feat * times, jnp.broadcast_to(times, feat.shape)], axis=1)
        offset = height if side == 1 else -height
        weights = cell_weights(factor, row_ref, [float(offset + i) for i in range(height)])
        total = dot(weights, values.astype(BF16))
        where = jnp.where(s_ref[2] == side, 0, 1)
        out_ref[where, : height * width] = total[:, :channels].astype(BF16)
        for i in range(height):
            turned = total[i * width : (i + 1) * width, channels:].T[:16]
            out_ref[where, height * width + 16 * i : height * width + 16 * (i + 1)] = turned.astype(BF16)


def own_kernel(height, width, s_ref, feat_ref, row_ref, col_ref, numer_ref, denom_ref):
    slots, channels = feat_ref.shape
    live = lax.broadcasted_iota(jnp.int32, (slots, channels), 0) < s_ref[1]
    values = jnp.concatenate([jnp.where(live, feat_ref[...], 0.0), live.astype(F32)], axis=1)
    weights = cell_weights(column_factor(col_ref, width), row_ref, [float(i) for i in range(height)])
    total = dot(weights, values.astype(BF16))
    numer_ref[...] = total[:, :channels]
    denom_ref[...] = total[:, channels:]


def partners(s_ref):
    first = jnp.where(s_ref[2] == 1, s_ref[4], s_ref[3])
    second = jnp.where(s_ref[2] == 1, s_ref[3], s_ref[4])
    return first, second


def finish_kernel(height, width, s_ref, numer_ref, denom_ref, first_ref, second_ref, out_ref):
    first, second = partners(s_ref)
    cells = height * width

    def got(part):
        return jnp.where(first == 1, first_ref[part].astype(F32), 0.0) + jnp.where(
            second == 1, second_ref[part].astype(F32), 0.0
        )

    for i in range(height):
        rows = slice(i * width, (i + 1) * width)
        added = got(slice(cells + 16 * i, cells + 16 * i + 16))[:1]
        added = jnp.broadcast_to(added, (width, width)).T[:, : numer_ref.shape[1]]
        numer = numer_ref[rows] + got(rows)
        out_ref[rows] = (numer * lax.rsqrt(1.0 + denom_ref[rows] + added)).astype(BF16)


def side_rows(s_ref, first_ref, second_ref):
    up = s_ref[2] == 1
    first, second = first_ref[...], second_ref[...]
    none = jnp.zeros_like(first)
    below = jnp.where(s_ref[3] == 1, jnp.where(up, second, first), none)
    above = jnp.where(s_ref[4] == 1, jnp.where(up, first, second), none)
    return below, above


def first_kernel(height, width, offsets, s_ref, own_ref, a_ref, b_ref, w_ref, pre_ref, sent_ref, edge_ref, w_full):
    cells, channels = own_ref.shape
    hidden = w_ref.shape[2]
    piece = w_ref.shape[1]
    for place, offset in enumerate(offsets):
        at = lax.bitwise_xor(s_ref[5], offset) * piece
        w_full[pl.ds(pl.multiple_of(at, 32), piece)] = w_ref[place]
    below, above = side_rows(s_ref, a_ref, b_ref)
    grid = jnp.concatenate([below[-2 * width :], own_ref[...], above[: 2 * width]], axis=0)
    rows = height + 2
    moved = [shifted(grid, step, width) for step in (-1, 0, 1)]
    patches = jnp.concatenate([moved[dx][dy * width : (dy + rows) * width] for dy in range(3) for dx in range(3)], axis=1)
    pre = dot(patches, w_full[...])
    h1 = pre * jax.nn.sigmoid(pre)
    h1 = h1.astype(BF16)
    zero = jnp.zeros((width, hidden), BF16)
    low = jnp.where(s_ref[3] == 1, h1[:width], zero)
    high = jnp.where(s_ref[4] == 1, h1[-width:], zero)
    middle = h1[width:-width]
    pre_ref[...] = pre[width:-width]
    sent_ref[:cells] = middle
    near = grid[width:-width]
    for i in range(rows):
        sent_ref[cells:, i * channels : (i + 1) * channels] = near[i * width : (i + 1) * width]
    edge_ref[:width] = low
    edge_ref[width:] = high


def chunk_place(s_ref, step, per_group, per_block):
    chunk = s_ref[6] * per_group + step
    block = chunk // per_block
    return block // 3, block % 3, chunk % per_block


def back_kernel(height, width, chunk, s_ref, *refs):
    count = (len(refs) - 2) // 2
    grids, w_ref, outs, (moved_ref,) = refs[:count], refs[count], refs[count + 1 : -1], refs[-1:]
    hidden = w_ref.shape[1]
    halves = hidden // chunk
    cells = height * width
    per_group = w_ref.shape[0] // chunk
    for member, (grid_ref, out_ref) in enumerate(zip(grids, outs)):
        grid = grid_ref[...]
        for dx in range(3):
            moved_ref[member, dx] = shifted(grid, 1 - dx, width)
        totals = [jnp.zeros((cells, chunk), F32) for _ in range(halves)]
        for step in range(per_group):
            dy, dx, half = chunk_place(s_ref, step, per_group, halves)
            rows = pl.ds(pl.multiple_of((2 - dy) * width, width), cells)
            totals[step % halves] += dot_nt(moved_ref[member, dx, rows], w_ref[step * chunk : (step + 1) * chunk])
        start = chunk_place(s_ref, 0, per_group, halves)[2]
        for rank in range(halves):
            half = lax.rem(start + rank, halves)
            columns = pl.ds(pl.multiple_of(half * chunk, chunk), chunk)
            out_ref[:, columns] = totals[rank].astype(out_ref.dtype)


def second_kernel(height, width, chunk, s_ref, *refs):
    count = (len(refs) - 2) // 3
    w_ref, outs, (moved_ref,) = refs[2 * count], refs[2 * count + 1 : -1], refs[-1:]
    hidden = w_ref.shape[1]
    halves = hidden // chunk
    cells = height * width
    per_group = w_ref.shape[0] // chunk
    for member in range(count):
        mid_ref, edge_ref, out_ref = refs[member], refs[count + member], outs[member]
        grid = jnp.concatenate([edge_ref[:width], mid_ref[:cells], edge_ref[width:]], axis=0)
        for dx in range(3):
            place = shifted(grid, dx - 1, width)
            for half in range(halves):
                moved_ref[member, dx, half] = place[:, half * chunk : (half + 1) * chunk]
        total = mid_ref[:cells].astype(F32) if member == 0 else jnp.zeros((cells, hidden), F32)
        for step in range(per_group):
            dy, dx, half = chunk_place(s_ref, step, per_group, halves)
            rows = pl.ds(pl.multiple_of(dy * width, width), cells)
            total += dot(moved_ref[member, dx, half, rows], w_ref[step * chunk : (step + 1) * chunk])
        out_ref[...] = total.astype(out_ref.dtype)


def dpre_kernel(s_ref, pre_ref, cot_ref, *refs):
    parts, out_ref = refs[:-1], refs[-1]
    pre = pre_ref[...]
    back = cot_ref[...].astype(F32)
    for part in parts:
        back = back + part[...].astype(F32)
    sig = jax.nn.sigmoid(pre)
    out_ref[...] = (back * sig * (1.0 + pre * (1.0 - sig))).T.astype(BF16)


def turn_kernel(height, width, rows_out, blocks, s_ref, cot_ref, out_ref):
    times, _, hidden = cot_ref.shape
    cells = height * width
    first = (s_ref[5] * rows_out) // hidden
    for j in range(blocks):
        block = jnp.minimum(first + j, 8)
        dy, dx = block // 3, block % 3
        rows = pl.ds(pl.multiple_of((2 - dy) * width, width), cells)
        for t in range(times):
            x = shifted(cot_ref[t, rows], 1 - dx, width)
            out_ref[j, :, t * cells : (t + 1) * cells] = x.astype(F32).T.astype(BF16)


def grad_second_kernel(cells, rows_out, blocks, s_ref, turned_ref, h1_ref, out_ref, full_ref):
    times, _, hidden = h1_ref.shape
    base = s_ref[5] * rows_out
    off = base - (base // hidden) * hidden
    h1 = h1_ref[:, :cells].reshape(times * cells, hidden)
    for j in range(blocks):
        full_ref[:, j * hidden : (j + 1) * hidden] = dot(turned_ref[j], h1)
    lats, part, _ = out_ref.shape
    columns = pl.ds(pl.multiple_of(off, 128), rows_out)
    for k in range(lats):
        at = lax.bitwise_xor(s_ref[0], k) * part
        out_ref[k] = full_ref[pl.ds(pl.multiple_of(at, part), part), columns].astype(BF16)


def grad_first_kernel(height, width, rows_out, blocks, s_ref, dpre_ref, sent_ref, out_ref, full_ref):
    times, hidden, cells = dpre_ref.shape
    rows = height + 2
    channels = sent_ref.shape[2] // rows
    base = s_ref[5] * rows_out
    first = base // channels
    off = base - first * channels
    total = jnp.zeros((hidden, blocks * channels), F32)
    for t in range(times):
        grid = jnp.concatenate([sent_ref[t, cells:, i * channels : (i + 1) * channels] for i in range(rows)], axis=0)
        full_ref[t] = grid
        pieces = []
        for j in range(blocks):
            block = jnp.minimum(first + j, 8)
            dy, dx = block // 3, block % 3
            near = full_ref[t, pl.ds(pl.multiple_of(dy * width, width), cells)]
            pieces.append(shifted(near, dx - 1, width))
        total += dot(dpre_ref[t], jnp.concatenate(pieces, axis=1))
    wide = blocks * channels
    total = pltpu.roll(total, lax.rem(wide - off, wide), 1)[:, :rows_out].astype(BF16)
    lats, part, _ = out_ref.shape
    for k in range(lats):
        out_ref[lax.bitwise_xor(s_ref[0], k)] = total[k * part : (k + 1) * part]


def swap(value, axis, bit):
    return lax.ppermute(value, axis, [(i, i ^ bit) for i in range(lax.axis_size(axis))])


def gathered(value, axis, bits):
    value = value[None]
    for bit in bits:
        value = jnp.concatenate([value, swap(value, axis, bit)], axis=0)
    return value


def distances(bits):
    order = [0]
    for bit in bits:
        order = order + [n ^ bit for n in order]
    return order


def with_partners(first, second):
    size = lax.axis_size("lat")
    pairs = [(i, i + 1) for i in range(1, size - 1, 2)]
    pairs = pairs + [(j, i) for i, j in pairs] + [(0, 0), (size - 1, size - 1)]
    return swap(first, "lat", 1), lax.ppermute(second, "lat", pairs)


def split_by(value, offsets, bit):
    keep = [n for n, k in enumerate(offsets) if not k & bit]
    send = [n for n, k in enumerate(offsets) if k & bit]
    pick = lambda places: jnp.concatenate([value[n : n + 1] for n in places], axis=0)
    return pick(keep), pick(send), [offsets[n] for n in keep]


def lat_step(value, offsets, bit):
    keep, send, offsets = split_by(value, offsets, bit)
    got = swap(send, "lat", bit)
    return (keep.astype(F32) + got.astype(F32)).astype(BF16), offsets


def lat_sum(value):
    size = value.shape[0]
    bits = [1 << n for n in range(size.bit_length() - 1)]
    half = value.shape[1] // 2
    one, two = value[:, :half], value[:, half:]
    offs_one = offs_two = list(range(size))
    for first, second in zip(bits[:1] + bits[1:2], bits[1:2] + bits[:1]):
        one, offs_one = lat_step(one, offs_one, first)
        two, offs_two = lat_step(two, offs_two, second)
    both = jnp.concatenate([one, two], axis=1)
    for bit in bits[2:-1]:
        both, offs_one = lat_step(both, offs_one, bit)
    keep, send, _ = split_by(both, offs_one, bits[-1])
    return keep[0].astype(F32) + swap(send, "lat", bits[-1])[0].astype(F32)


def small_lat_sum(value):
    size = value.shape[0]
    bits = [1 << n for n in range(size.bit_length() - 1)]
    offsets = list(range(size))
    for bit in bits[:-1]:
        value, offsets = lat_step(value, offsets, bit)
    keep, send, _ = split_by(value, offsets, bits[-1])
    return keep[0].astype(F32) + swap(send, "lat", bits[-1])[0].astype(F32)


def local(obs_feat, obs_row, obs_col, counts, edge_index, edge_mask, cotangent, w_first, w_second):
    _, height, width, hidden = cotangent.shape
    channels = obs_feat.shape[2]
    cells = height * width
    n_dp, n_lat = lax.axis_size("dp"), lax.axis_size("lat")
    band, member = lax.axis_index("lat"), lax.axis_index("dp")
    group = member // 2
    scalars = jnp.stack(
        [
            band,
            counts[0, 0],
            1 - band % 2,
            (band > 0).astype(jnp.int32),
            (band < n_lat - 1).astype(jnp.int32),
            member,
            group,
        ]
    ).astype(jnp.int32)
    bits = [1 << n for n in reversed(range(n_dp.bit_length() - 1))]
    outer = bits[:-1]
    up = scalars[2] == 1
    cot = cotangent[0].reshape(cells, hidden)

    w_one = gathered(w_first, "dp", bits)
    w_other = swap(w_second, "dp", 1)
    lower = member % 2 == 0
    w_two = jnp.concatenate([jnp.where(lower, w_second, w_other), jnp.where(lower, w_other, w_second)], axis=0)

    feat, row, col = obs_feat[0], obs_row, obs_col
    payload = height * (width + 16)
    edges = call(
        functools.partial(edge_kernel, height, width), "edges", [like((2, payload, channels), BF16)], flops=2**28
    )(scalars, feat, row, col, edge_index[0, 0], edge_mask[0, 0])[0]
    from_first, from_second = with_partners(edges[0], edges[1])
    numer, denom = call(
        functools.partial(own_kernel, height, width), "own", [like((cells, channels), F32)] * 2, flops=2**28
    )(scalars, feat, row, col)
    h0 = call(functools.partial(finish_kernel, height, width), "finish", [like((cells, channels), BF16)], flops=2**20)(
        scalars, numer, denom, from_first, from_second
    )[0]
    h0_first, h0_second = with_partners(h0, h0)

    low, high = cot[:width], cot[-width:]
    cot_first, cot_second = with_partners(jnp.where(up, high, low), jnp.where(up, low, high))
    none = jnp.zeros_like(low)
    below = jnp.where(scalars[3] == 1, jnp.where(up, cot_second, cot_first), none)
    above = jnp.where(scalars[4] == 1, jnp.where(up, cot_first, cot_second), none)
    cot_wide = jnp.concatenate([below, cot, above], axis=0)
    cot_near = gathered(cot_wide, "dp", outer)
    cot_all = jnp.concatenate([cot_near, swap(cot_near, "dp", 1)], axis=0)

    chunk = math.gcd(w_two.shape[0], hidden)
    near = cot_near.shape[0]
    wide_cells = (height + 2) * width
    backs = call(
        functools.partial(back_kernel, height, width, chunk),
        "back",
        [like((cells, hidden), F32)] + [like((cells, hidden), BF16)] * (near - 1),
        scratch=[pltpu.VMEM((near, 3, wide_cells, hidden), BF16)],
        flops=2 * near * cells * w_two.shape[0] * hidden,
    )(scalars, *[cot_near[n] for n in range(near)], w_two)
    away = distances(outer)
    backs = [backs[0]] + [swap(backs[n], "dp", away[n]) for n in range(1, near)]

    pre1, sent, edge = call(
        functools.partial(first_kernel, height, width, distances(bits)),
        "first",
        [
            like((cells, hidden), F32),
            like((cells + width * (height + 2) * channels // hidden, hidden), BF16),
            like((2 * width, hidden), BF16),
        ],
        scratch=[pltpu.VMEM((n_dp * w_first.shape[0], hidden), BF16)],
        flops=4 * cells * 9 * channels * hidden,
    )(scalars, h0, h0_first, h0_second, w_one)
    sent_all = gathered(sent, "dp", bits)
    dpre = call(dpre_kernel, "dpre", [like((hidden, cells), BF16)], flops=2**22)(scalars, pre1, cot, *backs)[0]
    dpre_all = gathered(dpre, "dp", bits)

    rows_two, rows_one = w_second.shape[0], w_first.shape[0]
    blocks_two = max((d * rows_two + rows_two - 1) // hidden - d * rows_two // hidden + 1 for d in range(n_dp))
    blocks_one = max((d * rows_one + rows_one - 1) // channels - d * rows_one // channels + 1 for d in range(n_dp))
    part = hidden // n_lat
    turned = call(
        functools.partial(turn_kernel, height, width, rows_two, blocks_two),
        "turn",
        [like((blocks_two, hidden, n_dp * cells), BF16)],
        flops=2**26,
    )(scalars, cot_all)[0]
    grad_two = call(
        functools.partial(grad_second_kernel, cells, rows_two, blocks_two),
        "gradsecond",
        [like((n_lat, part, rows_two), BF16)],
        scratch=[pltpu.VMEM((hidden, blocks_two * hidden), F32)],
        flops=2 * blocks_two * hidden * hidden * n_dp * cells,
    )(scalars, turned, sent_all)[0]
    grad_second = lat_sum(grad_two).T
    grad_one = call(
        functools.partial(grad_first_kernel, height, width, rows_one, blocks_one),
        "gradfirst",
        [like((n_lat, part, rows_one), BF16)],
        scratch=[pltpu.VMEM((n_dp, wide_cells, channels), BF16)],
        flops=2 * blocks_one * channels * hidden * n_dp * cells,
    )(scalars, dpre_all, sent_all)[0]
    grad_first = small_lat_sum(grad_one).T

    edge_near = gathered(edge, "dp", outer)
    seconds = call(
        functools.partial(second_kernel, height, width, chunk),
        "second",
        [like((cells, hidden), F32)] + [like((cells, hidden), BF16)] * (near - 1),
        scratch=[pltpu.VMEM((near, 3, hidden // chunk, wide_cells, chunk), BF16)],
        flops=2 * near * cells * w_two.shape[0] * hidden,
    )(scalars, *[sent_all[n] for n in range(near)], *[edge_near[n] for n in range(near)], w_two)
    encoded = seconds[0]
    for n in range(1, near):
        encoded = encoded + swap(seconds[n], "dp", away[n]).astype(F32)
    encoded = encoded.astype(BF16).reshape(1, height, width, hidden)
    return encoded, grad_first, grad_second


def with_halo(value, sides, width):
    for axis, dim in sides:
        size, length = (lax.axis_size(axis), value.shape[dim])
        up = [(i, (i + 1) % size) for i in range(size - 1)]
        down = [(j, i) for i, j in up]
        last = lax.slice_in_dim(value, length - width, length, axis=dim)
        first = lax.slice_in_dim(value, 0, width, axis=dim)
        before = lax.ppermute(last, axis, up)
        after = lax.ppermute(first, axis, down)
        value = jnp.concatenate([before, value, after], axis=dim)
    return value


def passed_along(block, axis, distance):
    devices = range(lax.axis_size(axis))
    route = [(i - distance, i) for i in devices if i - distance in devices]
    return lax.ppermute(block, axis, route)


def gauss_weights(cell_rows, cell_cols, rows, cols, valid):
    drow = cell_rows[:, None] - rows[None, :]
    dcol = cell_cols[:, None] - cols[None, :]
    return valid[None, :] * jnp.exp(-0.5 * (drow * drow + dcol * dcol))


def haloed_rows(grid):
    padded = with_halo(grid, (("lat", 0),), 1)
    return jnp.pad(padded, ((0, 0), (1, 1), (0, 0)))


def padded_patches(padded, height, width):
    pieces = [padded[dy : dy + height, dx : dx + width] for dy in range(3) for dx in range(3)]
    return jnp.concatenate(pieces, axis=-1).reshape(height * width, -1)


def plain(obs_feat, obs_row, obs_col, counts, edge_index, edge_mask, cotangent, w_first, w_second):
    feat = obs_feat[0]
    slot_total = feat.shape[0]
    channels = feat.shape[1]
    height = cotangent.shape[1]
    width = cotangent.shape[2]
    hidden = cotangent.shape[3]
    band_index = lax.axis_index("lat")
    band_base = (band_index * height).astype(jnp.float32)
    count = counts[0, 0]
    row_g = obs_row[0] + band_base
    col_b = obs_col[0]
    slots = jnp.arange(slot_total, dtype=jnp.int32)
    valid = (slots < count).astype(jnp.float32)

    def pick(listed, listed_mask):
        picked_feat = jnp.take(feat, listed, axis=0)
        live_flag = listed_mask.astype(jnp.float32) * (listed < count).astype(jnp.float32)
        place = jnp.stack([jnp.take(row_g, listed), jnp.take(col_b, listed), live_flag], axis=1)
        return (picked_feat, place)

    low_feat, low_place = pick(edge_index[0, 0, 0], edge_mask[0, 0, 0])
    high_feat, high_place = pick(edge_index[0, 0, 1], edge_mask[0, 0, 1])
    below_feat, below_place = passed_along((high_feat, high_place), "lat", 1)
    above_feat, above_place = passed_along((low_feat, low_place), "lat", -1)
    recv_feat = jnp.concatenate([below_feat, above_feat], 0)
    recv_place = jnp.concatenate([below_place, above_place], 0)
    cells = jnp.arange(height * width, dtype=jnp.int32)
    cell_rows = band_base + (cells // width).astype(jnp.float32)
    cell_cols = (cells % width).astype(jnp.float32)
    edge_weights = gauss_weights(
        cell_rows, cell_cols, recv_place[:, 0], recv_place[:, 1], recv_place[:, 2]
    )
    numer = jnp.dot(edge_weights, recv_feat, precision=lax.Precision.HIGHEST)
    denom = jnp.sum(edge_weights, 1)
    own_weights = gauss_weights(cell_rows, cell_cols, row_g, col_b, valid)
    numer = numer + jnp.dot(own_weights, feat, precision=lax.Precision.HIGHEST)
    denom = denom + jnp.sum(own_weights, 1)
    h0 = (
        (numer / jnp.sqrt(1.0 + denom)[:, None])
        .astype(jnp.bfloat16)
        .reshape(height, width, channels)
    )

    def fold_rows(patches, piece):
        return jnp.dot(patches, piece, preferred_element_type=jnp.float32)

    patches0 = padded_patches(haloed_rows(h0), height, width)
    pre1 = fold_rows(patches0, lax.all_gather(w_first, "dp", axis=0, tiled=True))
    h1 = jax.nn.silu(pre1).astype(jnp.bfloat16)
    patches1 = padded_patches(haloed_rows(h1.reshape(height, width, hidden)), height, width)
    pre2 = fold_rows(patches1, lax.all_gather(w_second, "dp", axis=0, tiled=True))
    encoded = (h1.astype(jnp.float32) + pre2).astype(jnp.bfloat16).reshape(1, height, width, hidden)
    cot = cotangent[0]
    cot_pad = haloed_rows(cot).reshape(-1, hidden)
    spread = lax.dot_general(
        cot_pad,
        lax.all_gather(w_second, "dp", axis=0, tiled=True),
        (((1,), (1,)), ((), ())),
        preferred_element_type=jnp.float32,
    )
    spread = spread.reshape(height + 2, width + 2, 9, hidden)
    dh1 = cot.astype(jnp.float32)
    for dy in range(3):
        for dx in range(3):
            dh1 = dh1 + spread[2 - dy : 2 - dy + height, 2 - dx : 2 - dx + width, dy * 3 + dx]
    sig = jax.nn.sigmoid(pre1)
    dpre1 = (dh1.reshape(-1, hidden) * sig * (1.0 + pre1 * (1.0 - sig))).astype(jnp.bfloat16)
    cot_flat = cot.reshape(-1, hidden)
    contract = (((0,), (0,)), ((), ()))
    grad_two = lax.dot_general(patches1, cot_flat, contract, preferred_element_type=jnp.float32)
    grad_one = lax.dot_general(patches0, dpre1, contract, preferred_element_type=jnp.float32)
    partial_one, partial_two = (
        lax.psum_scatter(
            grad_one.astype(jnp.bfloat16), "dp", scatter_dimension=0, tiled=True
        ).astype(jnp.float32),
        lax.psum_scatter(
            grad_two.astype(jnp.bfloat16), "dp", scatter_dimension=0, tiled=True
        ).astype(jnp.float32),
    )
    grad_first, grad_second = (
        lax.psum_scatter(
            partial_one.astype(jnp.bfloat16), "lat", scatter_dimension=1, tiled=True
        ).astype(jnp.float32),
        lax.psum_scatter(
            partial_two.astype(jnp.bfloat16), "lat", scatter_dimension=1, tiled=True
        ).astype(jnp.float32),
    )
    return (encoded, grad_first, grad_second)


def fits(mesh, height, width, hidden, channels, rows_one, rows_two):
    n_dp, n_lat = mesh.shape["dp"], mesh.shape["lat"]
    powers = all(n & (n - 1) == 0 for n in (n_dp, n_lat, hidden, channels))
    grid = height == 2 and width == channels and width % 128 == 0 and (height + 2) * channels == hidden
    return powers and grid and n_dp > 1 and n_lat > 4 and (hidden // n_lat) % 32 == 0 and rows_one % 32 == 0 and rows_two % 128 == 0


def solution(mesh):
    in_specs = (
        P("dp", "lat", None),
        P("dp", "lat"),
        P("dp", "lat"),
        P("dp", "lat"),
        P("dp", "lat", None, None),
        P("dp", "lat", None, None),
        P("dp", "lat", None, None),
        P("dp", None),
        P("dp", None),
    )
    out_specs = (P("dp", "lat", None, None), P("dp", "lat"), P("dp", "lat"))

    def run(*args):
        feat, cot, w_first, w_second = args[0], args[6], args[7], args[8]
        n_dp, n_lat = mesh.shape["dp"], mesh.shape["lat"]
        shapes = (cot.shape[1] // n_lat, *cot.shape[2:], feat.shape[2], w_first.shape[0] // n_dp, w_second.shape[0] // n_dp)
        step = local if fits(mesh, *shapes) else plain
        return jax.shard_map(step, mesh=mesh, in_specs=in_specs, out_specs=out_specs, check_vma=False)(*args)

    return run
```

```python
import functools
import math

import jax
import jax.numpy as jnp
from jax import lax
from jax.experimental import pallas as pl
from jax.experimental.pallas import tpu as pltpu
from jax.sharding import PartitionSpec as P

BF16 = jnp.bfloat16
F32 = jnp.float32
VMEM = pl.BlockSpec(memory_space=pltpu.VMEM)
SMEM = pl.BlockSpec(memory_space=pltpu.SMEM)
FAR = pl.BlockSpec(memory_space=pltpu.HBM)


def call(kernel, name, outs, scratch=(), scalars=1, far=0, grant=48):
    def run(*args):
        return pl.pallas_call(
            kernel,
            name=name,
            out_shape=outs,
            in_specs=[SMEM] * scalars + [VMEM] * (len(args) - scalars - far) + [FAR] * far,
            out_specs=[VMEM] * len(outs),
            scratch_shapes=list(scratch),
            compiler_params=pltpu.CompilerParams(vmem_limit_bytes=grant * 2**20),
        )(*args)

    return run


def like(shape, dtype):
    return jax.ShapeDtypeStruct(shape, dtype)


def dot(a, b):
    return jnp.dot(a, b, preferred_element_type=F32)


def dot_nt(a, b):
    return lax.dot_general(a, b, (((1,), (1,)), ((), ())), preferred_element_type=F32)


def shifted(x, step, width):
    if isinstance(step, int) and step == 0:
        return x
    total = x.shape[0]
    wide = pltpu.roll(x.astype(F32), lax.rem(total - step, total) if not isinstance(step, int) else (total - step) % total, 0)
    place = lax.broadcasted_iota(jnp.int32, x.shape, 0) % width + step
    return jnp.where((place >= 0) & (place < width), wide, 0.0).astype(x.dtype)


def column_factor(col_ref, width):
    cells = lax.broadcasted_iota(jnp.int32, (width, col_ref.shape[1]), 0).astype(F32)
    away = cells - col_ref[...]
    return jnp.exp(-0.5 * (away * away))


def cell_weights(factor, row_ref, rows):
    parts = []
    for row in rows:
        away = row - row_ref[...]
        parts.append((factor * jnp.exp(-0.5 * (away * away))).astype(BF16))
    return jnp.concatenate(parts, axis=0)


def edge_kernel(height, width, s_ref, *refs):
    far, (first_ref, second_ref), near, sems = refs[:5], refs[5:7], refs[7:12], refs[12]
    copies = [pltpu.make_async_copy(a, b, sems.at[n]) for n, (a, b) in enumerate(zip(far, near))]
    for copy in copies:
        copy.start()
    for copy in copies:
        copy.wait()
    feat_ref, row_ref, col_ref, index_ref, mask_ref = near
    slots, channels = feat_ref.shape
    factor = column_factor(col_ref, width)
    entries = index_ref.shape[1]
    slot = lax.broadcasted_iota(jnp.int32, (slots, entries), 0)
    live = slot < s_ref[1]
    feat = feat_ref[...]
    totals = []
    for side in range(2):
        named = jnp.where((slot == index_ref[side : side + 1]) & live, mask_ref[side : side + 1], 0)
        times = jnp.sum(named.astype(F32), axis=1, keepdims=True)
        values = jnp.concatenate([feat * times, jnp.broadcast_to(times, feat.shape)], axis=1)
        offset = height if side == 1 else -height
        weights = cell_weights(factor, row_ref, [float(offset + i) for i in range(height)])
        totals.append(dot(weights, values.astype(BF16)))
    for out_ref, one, other in ((first_ref, 1, 0), (second_ref, 0, 1)):
        total = jnp.where(s_ref[2] == 1, totals[one], totals[other])
        out_ref[: height * width] = total[:, :channels].astype(BF16)
        for i in range(height):
            turned = total[i * width : (i + 1) * width, channels:].T[:16]
            out_ref[height * width + 16 * i : height * width + 16 * (i + 1)] = turned.astype(BF16)


def own_kernel(height, width, s_ref, feat_ref, row_ref, col_ref, numer_ref, denom_ref):
    slots, channels = feat_ref.shape
    live = lax.broadcasted_iota(jnp.int32, (slots, channels), 0) < s_ref[1]
    values = jnp.concatenate([jnp.where(live, feat_ref[...], 0.0), live.astype(F32)], axis=1)
    weights = cell_weights(column_factor(col_ref, width), row_ref, [float(i) for i in range(height)])
    total = dot(weights, values.astype(BF16))
    numer_ref[...] = total[:, :channels]
    denom_ref[...] = total[:, channels:]


def partners(s_ref):
    first = jnp.where(s_ref[2] == 1, s_ref[4], s_ref[3])
    second = jnp.where(s_ref[2] == 1, s_ref[3], s_ref[4])
    return first, second


def finish_kernel(height, width, s_ref, numer_ref, denom_ref, first_ref, second_ref, out_ref):
    first, second = partners(s_ref)
    cells = height * width

    def got(part):
        return jnp.where(first == 1, first_ref[part].astype(F32), 0.0) + jnp.where(
            second == 1, second_ref[part].astype(F32), 0.0
        )

    for i in range(height):
        rows = slice(i * width, (i + 1) * width)
        added = got(slice(cells + 16 * i, cells + 16 * i + 16))[:1]
        added = jnp.broadcast_to(added, (width, width)).T[:, : numer_ref.shape[1]]
        numer = numer_ref[rows] + got(rows)
        out_ref[rows] = (numer * lax.rsqrt(1.0 + denom_ref[rows] + added)).astype(BF16)


def side_rows(s_ref, first, second):
    up = s_ref[2] == 1
    none = jnp.zeros_like(first)
    below = jnp.where(s_ref[3] == 1, jnp.where(up, second, first), none)
    above = jnp.where(s_ref[4] == 1, jnp.where(up, first, second), none)
    return below, above


def first_kernel(height, width, offsets, s_ref, own_ref, a_ref, b_ref, w_near, w_far, cot_ref, other_ref, *refs):
    pre_ref, h1_ref, edge_ref, near_ref, pair_ref, side_a, side_b, w_full = refs
    channels = own_ref.shape[1]
    count, piece, hidden = w_near.shape
    for place, offset in enumerate(offsets):
        at = lax.bitwise_xor(s_ref[5], offset) * piece
        w_full[pl.ds(pl.multiple_of(at, 32), piece)] = (w_near, w_far)[place // count][place % count]
    below, above = side_rows(s_ref, a_ref[...], b_ref[...])
    grid = jnp.concatenate([below[-2 * width :], own_ref[...], above[: 2 * width]], axis=0)
    rows = height + 2
    moved = [shifted(grid, step, width) for step in (-1, 0, 1)]
    patches = jnp.concatenate([moved[dx][dy * width : (dy + rows) * width] for dy in range(3) for dx in range(3)], axis=1)
    pre = dot(patches, w_full[...])
    h1 = (pre * jax.nn.sigmoid(pre)).astype(BF16)
    zero = jnp.zeros((width, hidden), BF16)
    pre_ref[...] = pre[width:-width]
    h1_ref[...] = h1[width:-width]
    edge_ref[:width] = jnp.where(s_ref[3] == 1, h1[:width], zero)
    edge_ref[width:] = jnp.where(s_ref[4] == 1, h1[-width:], zero)
    near = grid[width:-width]
    for i in range(rows):
        near_ref[:, i * channels : (i + 1) * channels] = near[i * width : (i + 1) * width]
    for n, ref in enumerate((cot_ref, other_ref)):
        pair_ref[n] = ref[...]
        low, high = ref[:width], ref[(height - 1) * width :]
        side_a[n * width : (n + 1) * width] = jnp.where(s_ref[2] == 1, high, low)
        side_b[n * width : (n + 1) * width] = jnp.where(s_ref[2] == 1, low, high)


def wide_rows(s_ref, width, pair_ref, a_ref, b_ref, n):
    rows = slice(n * width, (n + 1) * width)
    below, above = side_rows(s_ref, a_ref[rows], b_ref[rows])
    return jnp.concatenate([below, pair_ref[n], above], axis=0)


def chunk_place(s_ref, step, per_group, per_block):
    chunk = s_ref[6] * per_group + step
    block = chunk // per_block
    return block // 3, block % 3, chunk % per_block


def back_kernel(height, width, chunk, s_ref, pair_ref, a_ref, b_ref, w_ref, own_ref, other_ref, moved_ref):
    hidden = w_ref.shape[1]
    halves = hidden // chunk
    cells = height * width
    per_group = w_ref.shape[0] // chunk
    for member, out_ref in enumerate((own_ref, other_ref)):
        grid = wide_rows(s_ref, width, pair_ref, a_ref, b_ref, member)
        for dx in range(3):
            moved_ref[member, dx] = shifted(grid, 1 - dx, width)
        totals = [jnp.zeros((cells, chunk), F32) for _ in range(halves)]
        for step in range(per_group):
            dy, dx, _ = chunk_place(s_ref, step, per_group, halves)
            rows = pl.ds(pl.multiple_of((2 - dy) * width, width), cells)
            totals[step % halves] += dot_nt(moved_ref[member, dx, rows], w_ref[step * chunk : (step + 1) * chunk])
        start = chunk_place(s_ref, 0, per_group, halves)[2]
        for rank in range(halves):
            half = lax.rem(start + rank, halves)
            columns = pl.ds(pl.multiple_of(half * chunk, chunk), chunk)
            out_ref[:, columns] = totals[rank].astype(out_ref.dtype)


def second_kernel(height, width, chunk, s_ref, mid_one, mid_two, edge_one, edge_two, w_ref, own_ref, other_ref, moved_ref):
    hidden = w_ref.shape[1]
    halves = hidden // chunk
    cells = height * width
    per_group = w_ref.shape[0] // chunk
    for member, (mid_ref, edge_ref, out_ref) in enumerate(((mid_one, edge_one, own_ref), (mid_two, edge_two, other_ref))):
        grid = jnp.concatenate([edge_ref[:width], mid_ref[...], edge_ref[width:]], axis=0)
        for dx in range(3):
            place = shifted(grid, dx - 1, width)
            for half in range(halves):
                moved_ref[member, dx, half] = place[:, half * chunk : (half + 1) * chunk]
        total = mid_ref[...].astype(F32) if member == 0 else jnp.zeros((cells, hidden), F32)
        for step in range(per_group):
            dy, dx, half = chunk_place(s_ref, step, per_group, halves)
            rows = pl.ds(pl.multiple_of(dy * width, width), cells)
            total += dot(moved_ref[member, dx, half, rows], w_ref[step * chunk : (step + 1) * chunk])
        out_ref[...] = total.astype(out_ref.dtype)


def dpre_kernel(s_ref, pre_ref, cot_ref, near_ref, own_ref, got_ref, out_ref):
    pre = pre_ref[...]
    back = cot_ref[...].astype(F32) + own_ref[...] + got_ref[...].astype(F32)
    sig = jax.nn.sigmoid(pre)
    hidden, cells = pre.shape[1], pre.shape[0]
    out_ref[:hidden] = (back * sig * (1.0 + pre * (1.0 - sig))).T.astype(BF16)
    width = near_ref.shape[0]
    for half in range(near_ref.shape[1] // cells):
        out_ref[hidden + half * width : hidden + (half + 1) * width] = near_ref[:, half * cells : (half + 1) * cells]


def turn_kernel(height, width, rows_out, s_ref, near_pair, near_a, near_b, far_pair, far_a, far_b, out_ref, wide_ref):
    count, cells, hidden = near_pair.shape
    first = (s_ref[5] * rows_out) // hidden
    for t in range(2 * count):
        refs = (near_pair, near_a, near_b) if t < count else (far_pair, far_a, far_b)
        wide_ref[t] = wide_rows(s_ref, width, *refs, t % count)
    for dx in range(3):
        j = lax.rem(dx + 3 - lax.rem(first, 3), 3)
        dy = jnp.minimum(first + j, 8) // 3
        rows = pl.ds(pl.multiple_of((2 - dy) * width, width), cells)
        for t in range(2 * count):
            x = shifted(wide_ref[t, rows], 1 - dx, width)
            out_ref[j, :, t * cells : (t + 1) * cells] = x.astype(F32).T.astype(BF16)


def grad_second_kernel(rows_out, blocks, lats, s_ref, turned_ref, *refs):
    h1_refs, (keep_one, send_one, keep_two, send_two, full_ref) = refs[:-5], refs[-5:]
    hidden = h1_refs[0].shape[1]
    base = s_ref[5] * rows_out
    off = base - (base // hidden) * hidden
    h1 = jnp.concatenate([h1_ref[...] for h1_ref in h1_refs], axis=0)
    for j in range(blocks):
        full_ref[:, j * hidden : (j + 1) * hidden] = dot(turned_ref[j], h1)
    part = hidden // lats
    half = part // 2
    columns = pl.ds(pl.multiple_of(off, 128), rows_out)
    slots = [0] * 4
    for k in range(lats):
        at = lax.bitwise_xor(s_ref[0], k) * part
        for number, (keep_ref, send_ref, bit) in enumerate(((keep_one, send_one, 1), (keep_two, send_two, 2))):
            sent = 1 if k & bit else 0
            place = 2 * number + sent
            rows = pl.ds(pl.multiple_of(at + number * half, half), half)
            (keep_ref, send_ref)[sent][slots[place]] = full_ref[rows, columns].astype(BF16)
            slots[place] += 1


def grad_first_kernel(height, width, rows_out, lats, distance, s_ref, *refs):
    sent_refs, (keep_ref, send_ref, full_ref) = refs[:-3], refs[-3:]
    cells = sent_refs[0].shape[1]
    channels = full_ref.shape[2]
    rows = height + 2
    hidden = rows * channels
    wide = 3 * channels
    part = hidden // lats
    for t, sent_ref in enumerate(sent_refs):
        for i in range(rows):
            half, side = i // height, i % height
            full_ref[t, i * width : (i + 1) * width] = sent_ref[
                hidden + half * width : hidden + (half + 1) * width, side * channels : (side + 1) * channels
            ]
    for out_ref, away in ((send_ref, distance), (keep_ref, 0)):
        base = lax.bitwise_xor(s_ref[5], away) * rows_out
        first = base // channels
        off = base - first * channels
        turn = lax.rem(first, 3)
        total = jnp.zeros((hidden, wide), F32)
        for t, sent_ref in enumerate(sent_refs):
            pieces = []
            for dx in range(3):
                dy = jnp.minimum(first + lax.rem(dx + 3 - turn, 3), 8) // 3
                near = full_ref[t, pl.ds(pl.multiple_of(dy * width, width), cells)]
                pieces.append(shifted(near, dx - 1, width))
            total += dot(sent_ref[:hidden], jnp.concatenate(pieces, axis=1))
        total = pltpu.roll(total, lax.rem(2 * wide - off - turn * channels, wide), 1)[:, :rows_out].astype(BF16)
        for k in range(lats):
            out_ref[lax.bitwise_xor(s_ref[0], k)] = total[k * part : (k + 1) * part]


def add_kernel(places, *refs):
    count = len(places)
    for n, (stay, go) in enumerate(places):
        keep_ref, got_ref = refs[2 * n : 2 * n + 2]
        stay_ref, go_ref = refs[2 * (count + n) : 2 * (count + n) + 2]
        for out_ref, picked in ((stay_ref, stay), (go_ref, go)):
            for slot, place in enumerate(picked):
                out_ref[slot] = (keep_ref[place].astype(F32) + got_ref[place].astype(F32)).astype(BF16)


def meet_kernel(one_ref, got_one, two_ref, got_two, stay_ref, go_ref):
    half = one_ref.shape[1]
    for rows, keep_ref, got_ref in ((slice(0, half), one_ref, got_one), (slice(half, 2 * half), two_ref, got_two)):
        for place in range(keep_ref.shape[0]):
            out_ref = (stay_ref, go_ref)[place % 2]
            out_ref[place // 2, rows] = (keep_ref[place].astype(F32) + got_ref[place].astype(F32)).astype(BF16)


def last_kernel(keep_ref, got_ref, out_ref):
    out_ref[...] = keep_ref[0].astype(F32) + got_ref[0].astype(F32)


def swap(value, axis, bit):
    return lax.ppermute(value, axis, [(i, i ^ bit) for i in range(lax.axis_size(axis))])


def after(value, other):
    return lax.optimization_barrier((value, other))[0]


def distances(bits):
    order = [0]
    for bit in bits:
        order = order + [n ^ bit for n in order]
    return order


def with_partners(first, second):
    size = lax.axis_size("lat")
    pairs = [(i, i + 1) for i in range(1, size - 1, 2)]
    pairs = pairs + [(j, i) for i, j in pairs] + [(0, 0), (size - 1, size - 1)]
    return swap(first, "lat", 1), lax.ppermute(second, "lat", pairs)


def parted(offsets, bit):
    stay = [n for n, k in enumerate(offsets) if not k & bit]
    go = [n for n, k in enumerate(offsets) if k & bit]
    return (stay, go), [offsets[n] for n in stay]


def add_step(streams, offsets, bits):
    places, left = zip(*[parted(o, b) for o, b in zip(offsets, bits)])
    outs = [like((len(side), *keep.shape[1:]), BF16) for (keep, _), place in zip(streams, places) for side in place]
    flat = call(functools.partial(add_kernel, places), "add", outs, scalars=0)(*[v for pair in streams for v in pair])
    return [flat[n : n + 2] for n in range(0, len(flat), 2)], list(left)


def finished(stay, got, offsets, bits):
    for bit in bits:
        ((stay, go),), (offsets,) = add_step([(stay, got)], [offsets], [bit])
        got = swap(go, "lat", bit)
    return call(last_kernel, "last", [like(stay.shape[1:], F32)], scalars=0)(stay, got)[0].T


def local(obs_feat, obs_row, obs_col, counts, edge_index, edge_mask, cotangent, w_first, w_second):
    _, height, width, hidden = cotangent.shape
    channels = obs_feat.shape[2]
    cells = height * width
    n_dp, n_lat = lax.axis_size("dp"), lax.axis_size("lat")
    band, member = lax.axis_index("lat"), lax.axis_index("dp")
    scalars = jnp.stack(
        [
            band,
            counts[0, 0],
            1 - band % 2,
            (band > 0).astype(jnp.int32),
            (band < n_lat - 1).astype(jnp.int32),
            member,
            member // 2,
        ]
    ).astype(jnp.int32)
    lat_bits = [1 << n for n in range(n_lat.bit_length() - 1)]
    outer = n_dp // 2
    cot = cotangent[0].reshape(cells, hidden)

    feat, row, col = obs_feat[0], obs_row, obs_col
    payload = like((height * (width + 16), channels), BF16)
    observed = [feat, row, col, edge_index[0, 0], edge_mask[0, 0]]
    edges = call(
        functools.partial(edge_kernel, height, width),
        "edges",
        [payload, payload],
        scratch=[pltpu.VMEM(v.shape, v.dtype) for v in observed] + [pltpu.SemaphoreType.DMA((len(observed),))],
        far=len(observed),
        grant=60,
    )(scalars, *observed)
    w_got, cot_got = swap(w_first, "dp", outer), swap(cot, "dp", outer)
    from_first, from_second = with_partners(*edges)
    numer, denom = call(functools.partial(own_kernel, height, width), "own", [like((cells, channels), F32)] * 2)(
        after(scalars, edges[0]), feat, row, col
    )
    h0 = call(functools.partial(finish_kernel, height, width), "finish", [like((cells, channels), BF16)])(
        after(scalars, w_got), numer, denom, from_first, from_second
    )[0]
    h0_first, h0_second = with_partners(h0, h0)

    w_near = jnp.stack([w_first, w_got])
    w_far = swap(w_near, "dp", 1)
    w_other = swap(after(w_second, h0), "dp", 1)
    side = like((2 * width, hidden), BF16)
    pre1, h1, edge, h0_near, cot_pair, side_a, side_b = call(
        functools.partial(first_kernel, height, width, distances([outer, 1])),
        "first",
        [
            like((cells, hidden), F32),
            like((cells, hidden), BF16),
            side,
            like((width, (height + 2) * channels), BF16),
            like((2, cells, hidden), BF16),
            side,
            side,
        ],
        scratch=[pltpu.VMEM((n_dp * w_first.shape[0], hidden), BF16)],
    )(after(scalars, w_other), h0, h0_first, h0_second, w_near, w_far, cot, cot_got)

    lower = member % 2 == 0
    w_other = after(w_other, h1)
    w_two = jnp.concatenate([jnp.where(lower, w_second, w_other), jnp.where(lower, w_other, w_second)], axis=0)
    h1_got = swap(h1, "dp", outer)
    got_a, got_b = with_partners(side_a, side_b)
    pair_far = swap(cot_pair, "dp", 1)
    h1_got, got_a, got_b, pair_far, w_two = lax.optimization_barrier((h1_got, got_a, got_b, pair_far, w_two))
    chunk = math.gcd(w_two.shape[0], hidden)
    wide_cells = (height + 2) * width
    partial_outs = [like((cells, hidden), F32), like((cells, hidden), BF16)]
    back, back_other = call(
        functools.partial(back_kernel, height, width, chunk),
        "back",
        partial_outs,
        scratch=[pltpu.VMEM((2, 3, wide_cells, hidden), BF16)],
    )(scalars, cot_pair, got_a, got_b, w_two)
    back_got = swap(back_other, "dp", outer)
    h1_far, h1_far_got, far_a, far_b = [swap(v, "dp", 1) for v in (h1, h1_got, got_a, got_b)]

    rows_two, rows_one = w_second.shape[0], w_first.shape[0]
    part = hidden // n_lat
    turned = call(
        functools.partial(turn_kernel, height, width, rows_two),
        "turn",
        [like((3, hidden, n_dp * cells), BF16)],
        scratch=[pltpu.VMEM((n_dp, wide_cells, hidden), BF16)],
    )(after(scalars, back), cot_pair, got_a, got_b, pair_far, far_a, far_b)[0]
    piece = like((n_lat // 2, part // 2, rows_two), BF16)
    keep_one, send_one, keep_two, send_two = call(
        functools.partial(grad_second_kernel, rows_two, 3, n_lat),
        "gradsecond",
        [piece] * 4,
        scratch=[pltpu.VMEM((hidden, 3 * hidden), F32)],
    )(scalars, turned, h1, h1_got, h1_far, h1_far_got)
    streams = [(keep_one, swap(send_one, "lat", 1)), (keep_two, swap(send_two, "lat", 2))]
    offsets = [[k for k in range(n_lat) if not k & bit] for bit in (1, 2)]
    ((stay_one, go_one), (stay_two, go_two)), _ = add_step(streams, offsets, (2, 1))
    got_one, got_two = swap(go_one, "lat", 2), swap(go_two, "lat", 1)
    stay, go = call(meet_kernel, "meet", [like((n_lat // 8, part, rows_two), BF16)] * 2, scalars=0)(
        stay_one, got_one, stay_two, got_two
    )
    grad_second = finished(stay, swap(go, "lat", 4), list(range(0, n_lat, 8)), lat_bits[3:])

    sent = call(dpre_kernel, "dpre", [like((hidden + (height + 2) // height * width, cells), BF16)])(
        after(scalars, keep_one), pre1, cot, h0_near, back, back_got
    )[0]
    keep, send = call(
        functools.partial(grad_first_kernel, height, width, rows_one, n_lat, outer),
        "gradfirst",
        [like((n_lat, part, rows_one), BF16)] * 2,
        scratch=[pltpu.VMEM((2, wide_cells, channels), BF16)],
    )(scalars, sent, swap(sent, "dp", 1))
    grad_first = finished(keep, swap(send, "dp", outer), list(range(n_lat)), lat_bits)

    edge_got = swap(after(edge, send_one), "dp", outer)
    second, second_other = call(
        functools.partial(second_kernel, height, width, chunk),
        "second",
        partial_outs,
        scratch=[pltpu.VMEM((2, 3, hidden // chunk, wide_cells, chunk), BF16)],
    )(scalars, h1, h1_got, edge, edge_got, w_two)
    encoded = (second + swap(second_other, "dp", outer).astype(F32)).astype(BF16).reshape(1, height, width, hidden)
    return encoded, grad_first, grad_second


def with_halo(value, sides, width):
    for axis, dim in sides:
        size, length = (lax.axis_size(axis), value.shape[dim])
        up = [(i, (i + 1) % size) for i in range(size - 1)]
        down = [(j, i) for i, j in up]
        last = lax.slice_in_dim(value, length - width, length, axis=dim)
        first = lax.slice_in_dim(value, 0, width, axis=dim)
        before = lax.ppermute(last, axis, up)
        after = lax.ppermute(first, axis, down)
        value = jnp.concatenate([before, value, after], axis=dim)
    return value


def passed_along(block, axis, distance):
    devices = range(lax.axis_size(axis))
    route = [(i - distance, i) for i in devices if i - distance in devices]
    return lax.ppermute(block, axis, route)


def gauss_weights(cell_rows, cell_cols, rows, cols, valid):
    drow = cell_rows[:, None] - rows[None, :]
    dcol = cell_cols[:, None] - cols[None, :]
    return valid[None, :] * jnp.exp(-0.5 * (drow * drow + dcol * dcol))


def haloed_rows(grid):
    padded = with_halo(grid, (("lat", 0),), 1)
    return jnp.pad(padded, ((0, 0), (1, 1), (0, 0)))


def padded_patches(padded, height, width):
    pieces = [padded[dy : dy + height, dx : dx + width] for dy in range(3) for dx in range(3)]
    return jnp.concatenate(pieces, axis=-1).reshape(height * width, -1)


def plain(obs_feat, obs_row, obs_col, counts, edge_index, edge_mask, cotangent, w_first, w_second):
    feat = obs_feat[0]
    slot_total = feat.shape[0]
    channels = feat.shape[1]
    height = cotangent.shape[1]
    width = cotangent.shape[2]
    hidden = cotangent.shape[3]
    band_index = lax.axis_index("lat")
    band_base = (band_index * height).astype(jnp.float32)
    count = counts[0, 0]
    row_g = obs_row[0] + band_base
    col_b = obs_col[0]
    slots = jnp.arange(slot_total, dtype=jnp.int32)
    valid = (slots < count).astype(jnp.float32)

    def pick(listed, listed_mask):
        picked_feat = jnp.take(feat, listed, axis=0)
        live_flag = listed_mask.astype(jnp.float32) * (listed < count).astype(jnp.float32)
        place = jnp.stack([jnp.take(row_g, listed), jnp.take(col_b, listed), live_flag], axis=1)
        return (picked_feat, place)

    low_feat, low_place = pick(edge_index[0, 0, 0], edge_mask[0, 0, 0])
    high_feat, high_place = pick(edge_index[0, 0, 1], edge_mask[0, 0, 1])
    below_feat, below_place = passed_along((high_feat, high_place), "lat", 1)
    above_feat, above_place = passed_along((low_feat, low_place), "lat", -1)
    recv_feat = jnp.concatenate([below_feat, above_feat], 0)
    recv_place = jnp.concatenate([below_place, above_place], 0)
    cells = jnp.arange(height * width, dtype=jnp.int32)
    cell_rows = band_base + (cells // width).astype(jnp.float32)
    cell_cols = (cells % width).astype(jnp.float32)
    edge_weights = gauss_weights(
        cell_rows, cell_cols, recv_place[:, 0], recv_place[:, 1], recv_place[:, 2]
    )
    numer = jnp.dot(edge_weights, recv_feat, precision=lax.Precision.HIGHEST)
    denom = jnp.sum(edge_weights, 1)
    own_weights = gauss_weights(cell_rows, cell_cols, row_g, col_b, valid)
    numer = numer + jnp.dot(own_weights, feat, precision=lax.Precision.HIGHEST)
    denom = denom + jnp.sum(own_weights, 1)
    h0 = (
        (numer / jnp.sqrt(1.0 + denom)[:, None])
        .astype(jnp.bfloat16)
        .reshape(height, width, channels)
    )

    def fold_rows(patches, piece):
        return jnp.dot(patches, piece, preferred_element_type=jnp.float32)

    patches0 = padded_patches(haloed_rows(h0), height, width)
    pre1 = fold_rows(patches0, lax.all_gather(w_first, "dp", axis=0, tiled=True))
    h1 = jax.nn.silu(pre1).astype(jnp.bfloat16)
    patches1 = padded_patches(haloed_rows(h1.reshape(height, width, hidden)), height, width)
    pre2 = fold_rows(patches1, lax.all_gather(w_second, "dp", axis=0, tiled=True))
    encoded = (h1.astype(jnp.float32) + pre2).astype(jnp.bfloat16).reshape(1, height, width, hidden)
    cot = cotangent[0]
    cot_pad = haloed_rows(cot).reshape(-1, hidden)
    spread = lax.dot_general(
        cot_pad,
        lax.all_gather(w_second, "dp", axis=0, tiled=True),
        (((1,), (1,)), ((), ())),
        preferred_element_type=jnp.float32,
    )
    spread = spread.reshape(height + 2, width + 2, 9, hidden)
    dh1 = cot.astype(jnp.float32)
    for dy in range(3):
        for dx in range(3):
            dh1 = dh1 + spread[2 - dy : 2 - dy + height, 2 - dx : 2 - dx + width, dy * 3 + dx]
    sig = jax.nn.sigmoid(pre1)
    dpre1 = (dh1.reshape(-1, hidden) * sig * (1.0 + pre1 * (1.0 - sig))).astype(jnp.bfloat16)
    cot_flat = cot.reshape(-1, hidden)
    contract = (((0,), (0,)), ((), ()))
    grad_two = lax.dot_general(patches1, cot_flat, contract, preferred_element_type=jnp.float32)
    grad_one = lax.dot_general(patches0, dpre1, contract, preferred_element_type=jnp.float32)
    partial_one, partial_two = (
        lax.psum_scatter(
            grad_one.astype(jnp.bfloat16), "dp", scatter_dimension=0, tiled=True
        ).astype(jnp.float32),
        lax.psum_scatter(
            grad_two.astype(jnp.bfloat16), "dp", scatter_dimension=0, tiled=True
        ).astype(jnp.float32),
    )
    grad_first, grad_second = (
        lax.psum_scatter(
            partial_one.astype(jnp.bfloat16), "lat", scatter_dimension=1, tiled=True
        ).astype(jnp.float32),
        lax.psum_scatter(
            partial_two.astype(jnp.bfloat16), "lat", scatter_dimension=1, tiled=True
        ).astype(jnp.float32),
    )
    return (encoded, grad_first, grad_second)


def fits(mesh, height, width, hidden, channels, rows_one, rows_two):
    n_dp, n_lat = mesh.shape["dp"], mesh.shape["lat"]
    powers = all(n & (n - 1) == 0 for n in (n_dp, n_lat, hidden, channels))
    grid = height == 2 and width == channels and width % 128 == 0 and (height + 2) * channels == hidden
    blocks = all(
        [(d * rows + rows - 1) // size - d * rows // size for d in range(n_dp)] == [2] * n_dp
        for rows, size in ((rows_one, channels), (rows_two, hidden))
    )
    return powers and grid and n_dp == 2 * 2 and n_lat > 4 and (hidden // n_lat) % 32 == 0 and blocks and rows_one % 32 == 0 and rows_two % 128 == 0


def solution(mesh):
    in_specs = (
        P("dp", "lat", None),
        P("dp", "lat"),
        P("dp", "lat"),
        P("dp", "lat"),
        P("dp", "lat", None, None),
        P("dp", "lat", None, None),
        P("dp", "lat", None, None),
        P("dp", None),
        P("dp", None),
    )
    out_specs = (P("dp", "lat", None, None), P("dp", "lat"), P("dp", "lat"))

    def run(*args):
        feat, cot, w_first, w_second = args[0], args[6], args[7], args[8]
        n_dp, n_lat = mesh.shape["dp"], mesh.shape["lat"]
        shapes = (cot.shape[1] // n_lat, *cot.shape[2:], feat.shape[2], w_first.shape[0] // n_dp, w_second.shape[0] // n_dp)
        step = local if fits(mesh, *shapes) else plain
        return jax.shard_map(step, mesh=mesh, in_specs=in_specs, out_specs=out_specs, check_vma=False)(*args)

    return run
```

```python
import functools
import math

import jax
import jax.numpy as jnp
from jax import lax
from jax.experimental import pallas as pl
from jax.experimental.pallas import tpu as pltpu
from jax.sharding import PartitionSpec as P

BF16 = jnp.bfloat16
F32 = jnp.float32
VMEM = pl.BlockSpec(memory_space=pltpu.VMEM)
SMEM = pl.BlockSpec(memory_space=pltpu.SMEM)
FAR = pl.BlockSpec(memory_space=pltpu.HBM)


def call(kernel, name, outs, scratch=(), scalars=1, far=0, grant=48):
    def run(*args):
        return pl.pallas_call(
            kernel,
            name=name,
            out_shape=outs,
            in_specs=[SMEM] * scalars + [VMEM] * (len(args) - scalars - far) + [FAR] * far,
            out_specs=[VMEM] * len(outs),
            scratch_shapes=list(scratch),
            cost_estimate=pl.CostEstimate(flops=COST[name], bytes_accessed=0, transcendentals=0),
            compiler_params=pltpu.CompilerParams(vmem_limit_bytes=grant * 2**20),
        )(*args)

    return run


COST = {"edges": 4107269028, "own": 657163044, "finish": 1150035328, "back": 4600141312, "first": 24202651983, "turn": 2957233700, "gradsecond": 4107269028, "dpre": 1314326089, "gradfirst": 2464361417, "second": 4435850551, "add": 1150035328, "meet": 1150035328, "last": 1150035328}


def like(shape, dtype):
    return jax.ShapeDtypeStruct(shape, dtype)


def dot(a, b):
    return jnp.dot(a, b, preferred_element_type=F32)


def dot_nt(a, b):
    return lax.dot_general(a, b, (((1,), (1,)), ((), ())), preferred_element_type=F32)


def shifted(x, step, width):
    if isinstance(step, int) and step == 0:
        return x
    total = x.shape[0]
    wide = pltpu.roll(x.astype(F32), lax.rem(total - step, total) if not isinstance(step, int) else (total - step) % total, 0)
    place = lax.broadcasted_iota(jnp.int32, x.shape, 0) % width + step
    return jnp.where((place >= 0) & (place < width), wide, 0.0).astype(x.dtype)


def column_factor(col_ref, width):
    cells = lax.broadcasted_iota(jnp.int32, (width, col_ref.shape[1]), 0).astype(F32)
    away = cells - col_ref[...]
    return jnp.exp(-0.5 * (away * away))


def cell_weights(factor, row_ref, rows):
    parts = []
    for row in rows:
        away = row - row_ref[...]
        parts.append((factor * jnp.exp(-0.5 * (away * away))).astype(BF16))
    return jnp.concatenate(parts, axis=0)


def edge_kernel(height, width, s_ref, *refs):
    far, (first_ref, second_ref, side_a, side_b), near, sems = refs[:6], refs[6:10], refs[10:16], refs[16]
    copies = [pltpu.make_async_copy(a, b, sems.at[n]) for n, (a, b) in enumerate(zip(far, near))]
    for copy in copies:
        copy.start()
    for copy in copies:
        copy.wait()
    feat_ref, row_ref, col_ref, index_ref, mask_ref, cot_ref = near
    up = lax.rem(lax.axis_index("lat"), 2) == 0
    low, high = cot_ref[:width], cot_ref[(height - 1) * width :]
    side_a[...] = jnp.where(up, high, low)
    side_b[...] = jnp.where(up, low, high)
    slots, channels = feat_ref.shape
    factor = column_factor(col_ref, width)
    entries = index_ref.shape[1]
    slot = lax.broadcasted_iota(jnp.int32, (slots, entries), 0)
    live = slot < s_ref[0, 0]
    feat = feat_ref[...]
    totals = []
    for side in range(2):
        named = jnp.where((slot == index_ref[side : side + 1]) & live, mask_ref[side : side + 1], 0)
        times = jnp.sum(named.astype(F32), axis=1, keepdims=True)
        values = jnp.concatenate([feat * times, jnp.broadcast_to(times, feat.shape)], axis=1)
        offset = height if side == 1 else -height
        weights = cell_weights(factor, row_ref, [float(offset + i) for i in range(height)])
        totals.append(dot(weights, values.astype(BF16)))
    for out_ref, one, other in ((first_ref, 1, 0), (second_ref, 0, 1)):
        total = jnp.where(up, totals[one], totals[other])
        out_ref[: height * width] = total[:, :channels].astype(BF16)
        for i in range(height):
            turned = total[i * width : (i + 1) * width, channels:].T[:16]
            out_ref[height * width + 16 * i : height * width + 16 * (i + 1)] = turned.astype(BF16)


def own_kernel(height, width, s_ref, feat_ref, row_ref, col_ref, numer_ref, denom_ref):
    slots, channels = feat_ref.shape
    live = lax.broadcasted_iota(jnp.int32, (slots, channels), 0) < s_ref[0, 0]
    values = jnp.concatenate([jnp.where(live, feat_ref[...], 0.0), live.astype(F32)], axis=1)
    weights = cell_weights(column_factor(col_ref, width), row_ref, [float(i) for i in range(height)])
    total = dot(weights, values.astype(BF16))
    numer_ref[...] = total[:, :channels]
    denom_ref[...] = total[:, channels:]


def partners(s_ref):
    first = jnp.where(s_ref[2] == 1, s_ref[4], s_ref[3])
    second = jnp.where(s_ref[2] == 1, s_ref[3], s_ref[4])
    return first, second


def finish_kernel(height, width, s_ref, numer_ref, denom_ref, first_ref, second_ref, out_ref):
    first, second = partners(s_ref)
    cells = height * width

    def got(part):
        return jnp.where(first == 1, first_ref[part].astype(F32), 0.0) + jnp.where(
            second == 1, second_ref[part].astype(F32), 0.0
        )

    for i in range(height):
        rows = slice(i * width, (i + 1) * width)
        added = got(slice(cells + 16 * i, cells + 16 * i + 16))[:1]
        added = jnp.broadcast_to(added, (width, width)).T[:, : numer_ref.shape[1]]
        numer = numer_ref[rows] + got(rows)
        out_ref[rows] = (numer * lax.rsqrt(1.0 + denom_ref[rows] + added)).astype(BF16)


def side_rows(s_ref, first, second):
    up = s_ref[2] == 1
    none = jnp.zeros_like(first)
    below = jnp.where(s_ref[3] == 1, jnp.where(up, second, first), none)
    above = jnp.where(s_ref[4] == 1, jnp.where(up, first, second), none)
    return below, above


def first_kernel(height, width, offsets, s_ref, own_ref, a_ref, b_ref, w_near, w_far, *refs):
    pre_ref, h1_ref, edge_ref, near_ref, w_full = refs
    channels = own_ref.shape[1]
    count, piece, hidden = w_near.shape
    for place, offset in enumerate(offsets):
        at = lax.bitwise_xor(s_ref[5], offset) * piece
        w_full[pl.ds(pl.multiple_of(at, 32), piece)] = (w_near, w_far)[place // count][place % count]
    below, above = side_rows(s_ref, a_ref[...], b_ref[...])
    grid = jnp.concatenate([below[-2 * width :], own_ref[...], above[: 2 * width]], axis=0)
    rows = height + 2
    moved = [shifted(grid, step, width) for step in (-1, 0, 1)]
    patches = jnp.concatenate([moved[dx][dy * width : (dy + rows) * width] for dy in range(3) for dx in range(3)], axis=1)
    pre = dot(patches, w_full[...])
    h1 = (pre * jax.nn.sigmoid(pre)).astype(BF16)
    zero = jnp.zeros((width, hidden), BF16)
    pre_ref[...] = pre[width:-width]
    h1_ref[...] = h1[width:-width]
    edge_ref[:width] = jnp.where(s_ref[3] == 1, h1[:width], zero)
    edge_ref[width:] = jnp.where(s_ref[4] == 1, h1[-width:], zero)
    near = grid[width:-width]
    for i in range(rows):
        near_ref[:, i * channels : (i + 1) * channels] = near[i * width : (i + 1) * width]


def wide_rows(s_ref, width, cot_ref, side_ref):
    below, above = side_rows(s_ref, side_ref[:width], side_ref[width:])
    return jnp.concatenate([below, cot_ref[...], above], axis=0)


def chunk_place(s_ref, step, per_group, per_block):
    chunk = s_ref[6] * per_group + step
    block = chunk // per_block
    return block // 3, block % 3, chunk % per_block


def back_kernel(height, width, chunk, s_ref, cot_ref, cot_got, side_ref, side_got, w_ref, own_ref, other_ref, stack_ref, moved_ref):
    hidden = w_ref.shape[1]
    halves = hidden // chunk
    cells = height * width
    per_group = w_ref.shape[0] // chunk
    for place, ref in enumerate((cot_ref, cot_got, side_ref, side_got)):
        stack_ref[place] = ref[...]
    for member, out_ref in enumerate((own_ref, other_ref)):
        grid = wide_rows(s_ref, width, (cot_ref, cot_got)[member], (side_ref, side_got)[member])
        for dx in range(3):
            moved_ref[member, dx] = shifted(grid, 1 - dx, width)
        totals = [jnp.zeros((cells, chunk), F32) for _ in range(halves)]
        for step in range(per_group):
            dy, dx, _ = chunk_place(s_ref, step, per_group, halves)
            rows = pl.ds(pl.multiple_of((2 - dy) * width, width), cells)
            totals[step % halves] += dot_nt(moved_ref[member, dx, rows], w_ref[step * chunk : (step + 1) * chunk])
        start = chunk_place(s_ref, 0, per_group, halves)[2]
        for rank in range(halves):
            half = lax.rem(start + rank, halves)
            columns = pl.ds(pl.multiple_of(half * chunk, chunk), chunk)
            out_ref[:, columns] = totals[rank].astype(out_ref.dtype)


def second_kernel(height, width, chunk, s_ref, mid_one, mid_two, edge_one, edge_two, w_ref, own_ref, other_ref, moved_ref):
    hidden = w_ref.shape[1]
    halves = hidden // chunk
    cells = height * width
    per_group = w_ref.shape[0] // chunk
    for member, (mid_ref, edge_ref, out_ref) in enumerate(((mid_one, edge_one, own_ref), (mid_two, edge_two, other_ref))):
        grid = jnp.concatenate([edge_ref[:width], mid_ref[...], edge_ref[width:]], axis=0)
        for dx in range(3):
            place = shifted(grid, dx - 1, width)
            for half in range(halves):
                moved_ref[member, dx, half] = place[:, half * chunk : (half + 1) * chunk]
        total = mid_ref[...].astype(F32) if member == 0 else jnp.zeros((cells, hidden), F32)
        for step in range(per_group):
            dy, dx, half = chunk_place(s_ref, step, per_group, halves)
            rows = pl.ds(pl.multiple_of(dy * width, width), cells)
            total += dot(moved_ref[member, dx, half, rows], w_ref[step * chunk : (step + 1) * chunk])
        out_ref[...] = total.astype(out_ref.dtype)


def dpre_kernel(s_ref, pre_ref, cot_ref, near_ref, own_ref, got_ref, out_ref):
    pre = pre_ref[...]
    back = cot_ref[...].astype(F32) + own_ref[...] + got_ref[...].astype(F32)
    sig = jax.nn.sigmoid(pre)
    hidden, cells = pre.shape[1], pre.shape[0]
    out_ref[:hidden] = (back * sig * (1.0 + pre * (1.0 - sig))).T.astype(BF16)
    width = near_ref.shape[0]
    for half in range(near_ref.shape[1] // cells):
        out_ref[hidden + half * width : hidden + (half + 1) * width] = near_ref[:, half * cells : (half + 1) * cells]


def turn_kernel(height, width, rows_out, s_ref, *refs):
    near_ref, far_ref, out_ref, wide_ref = refs
    times, count = wide_ref.shape[0], wide_ref.shape[0] // 2
    _, cells, hidden = near_ref.shape
    first = (s_ref[5] * rows_out) // hidden
    for t in range(times):
        ref = (near_ref, far_ref)[t // count]
        wide_ref[t] = wide_rows(s_ref, width, ref.at[t % count], ref.at[count + t % count])
    for dx in range(3):
        j = lax.rem(dx + 3 - lax.rem(first, 3), 3)
        dy = jnp.minimum(first + j, 8) // 3
        rows = pl.ds(pl.multiple_of((2 - dy) * width, width), cells)
        for t in range(times):
            x = shifted(wide_ref[t, rows], 1 - dx, width)
            out_ref[j, :, t * cells : (t + 1) * cells] = x.astype(F32).T.astype(BF16)


def grad_second_kernel(rows_out, blocks, lats, s_ref, turned_ref, *refs):
    h1_refs, (keep_one, send_one, keep_two, send_two, full_ref) = refs[:-5], refs[-5:]
    hidden = h1_refs[0].shape[1]
    base = s_ref[5] * rows_out
    off = base - (base // hidden) * hidden
    h1 = jnp.concatenate([h1_ref[...] for h1_ref in h1_refs], axis=0)
    for j in range(blocks):
        full_ref[:, j * hidden : (j + 1) * hidden] = dot(turned_ref[j], h1)
    part = hidden // lats
    half = part // 2
    columns = pl.ds(pl.multiple_of(off, 128), rows_out)
    slots = [0] * 4
    for k in range(lats):
        at = lax.bitwise_xor(s_ref[0], k) * part
        for number, (keep_ref, send_ref, bit) in enumerate(((keep_one, send_one, 1), (keep_two, send_two, 2))):
            sent = 1 if k & bit else 0
            place = 2 * number + sent
            rows = pl.ds(pl.multiple_of(at + number * half, half), half)
            (keep_ref, send_ref)[sent][slots[place]] = full_ref[rows, columns].astype(BF16)
            slots[place] += 1


def grad_first_kernel(height, width, rows_out, lats, distance, s_ref, *refs):
    sent_refs, (keep_ref, send_ref, full_ref) = refs[:-3], refs[-3:]
    cells = sent_refs[0].shape[1]
    channels = full_ref.shape[2]
    rows = height + 2
    hidden = rows * channels
    wide = 3 * channels
    part = hidden // lats
    for t, sent_ref in enumerate(sent_refs):
        for i in range(rows):
            half, side = i // height, i % height
            full_ref[t, i * width : (i + 1) * width] = sent_ref[
                hidden + half * width : hidden + (half + 1) * width, side * channels : (side + 1) * channels
            ]
    for out_ref, away in ((send_ref, distance), (keep_ref, 0)):
        base = lax.bitwise_xor(s_ref[5], away) * rows_out
        first = base // channels
        off = base - first * channels
        turn = lax.rem(first, 3)
        total = jnp.zeros((hidden, wide), F32)
        for t, sent_ref in enumerate(sent_refs):
            pieces = []
            for dx in range(3):
                dy = jnp.minimum(first + lax.rem(dx + 3 - turn, 3), 8) // 3
                near = full_ref[t, pl.ds(pl.multiple_of(dy * width, width), cells)]
                pieces.append(shifted(near, dx - 1, width))
            total += dot(sent_ref[:hidden], jnp.concatenate(pieces, axis=1))
        total = pltpu.roll(total, lax.rem(2 * wide - off - turn * channels, wide), 1)[:, :rows_out].astype(BF16)
        for k in range(lats):
            out_ref[lax.bitwise_xor(s_ref[0], k)] = total[k * part : (k + 1) * part]


def add_kernel(places, *refs):
    count = len(places)
    for n, (stay, go) in enumerate(places):
        keep_ref, got_ref = refs[2 * n : 2 * n + 2]
        stay_ref, go_ref = refs[2 * (count + n) : 2 * (count + n) + 2]
        for out_ref, picked in ((stay_ref, stay), (go_ref, go)):
            for slot, place in enumerate(picked):
                out_ref[slot] = (keep_ref[place].astype(F32) + got_ref[place].astype(F32)).astype(BF16)


def meet_kernel(one_ref, got_one, two_ref, got_two, stay_ref, go_ref):
    half = one_ref.shape[1]
    for rows, keep_ref, got_ref in ((slice(0, half), one_ref, got_one), (slice(half, 2 * half), two_ref, got_two)):
        for place in range(keep_ref.shape[0]):
            out_ref = (stay_ref, go_ref)[place % 2]
            out_ref[place // 2, rows] = (keep_ref[place].astype(F32) + got_ref[place].astype(F32)).astype(BF16)


def last_kernel(keep_ref, got_ref, out_ref):
    out_ref[...] = keep_ref[0].astype(F32) + got_ref[0].astype(F32)


def swap(value, axis, bit):
    return lax.ppermute(value, axis, [(i, i ^ bit) for i in range(lax.axis_size(axis))])


def after(value, other):
    return lax.optimization_barrier((value, other))[0]


def distances(bits):
    order = [0]
    for bit in bits:
        order = order + [n ^ bit for n in order]
    return order


def with_partners(first, second):
    size = lax.axis_size("lat")
    pairs = [(i, i + 1) for i in range(1, size - 1, 2)]
    pairs = pairs + [(j, i) for i, j in pairs] + [(0, 0), (size - 1, size - 1)]
    return swap(first, "lat", 1), lax.ppermute(second, "lat", pairs)


def parted(offsets, bit):
    stay = [n for n, k in enumerate(offsets) if not k & bit]
    go = [n for n, k in enumerate(offsets) if k & bit]
    return (stay, go), [offsets[n] for n in stay]


def add_step(streams, offsets, bits):
    places, left = zip(*[parted(o, b) for o, b in zip(offsets, bits)])
    outs = [like((len(side), *keep.shape[1:]), BF16) for (keep, _), place in zip(streams, places) for side in place]
    flat = call(functools.partial(add_kernel, places), "add", outs, scalars=0)(*[v for pair in streams for v in pair])
    return [flat[n : n + 2] for n in range(0, len(flat), 2)], list(left)


def finished(stay, got, offsets, bits):
    for bit in bits:
        ((stay, go),), (offsets,) = add_step([(stay, got)], [offsets], [bit])
        got = swap(go, "lat", bit)
    return call(last_kernel, "last", [like(stay.shape[1:], F32)], scalars=0)(stay, got)[0].T


def local(obs_feat, obs_row, obs_col, counts, edge_index, edge_mask, cotangent, w_first, w_second):
    _, height, width, hidden = cotangent.shape
    channels = obs_feat.shape[2]
    cells = height * width
    n_dp, n_lat = lax.axis_size("dp"), lax.axis_size("lat")
    band, member = lax.axis_index("lat"), lax.axis_index("dp")
    scalars = jnp.stack(
        [
            band,
            counts[0, 0],
            1 - band % 2,
            (band > 0).astype(jnp.int32),
            (band < n_lat - 1).astype(jnp.int32),
            member,
            member // 2,
        ]
    ).astype(jnp.int32)
    lat_bits = [1 << n for n in range(n_lat.bit_length() - 1)]
    outer = n_dp // 2
    cot = cotangent[0].reshape(cells, hidden)

    feat, row, col = obs_feat[0], obs_row, obs_col
    payload = like((height * (width + 16), channels), BF16)
    observed = [feat, row, col, edge_index[0, 0], edge_mask[0, 0], cot]
    side = like((width, hidden), BF16)
    *edges, side_a, side_b = call(
        functools.partial(edge_kernel, height, width),
        "edges",
        [payload, payload, side, side],
        scratch=[pltpu.VMEM(v.shape, v.dtype) for v in observed] + [pltpu.SemaphoreType.DMA((len(observed),))],
        far=len(observed),
        grant=60,
    )(counts, *observed)
    cot_got, w_got, w_other = swap(cot, "dp", outer), swap(w_first, "dp", outer), swap(w_second, "dp", 1)
    side = jnp.concatenate(with_partners(side_a, side_b), axis=0)
    from_first, from_second = with_partners(*edges)
    numer, denom = call(functools.partial(own_kernel, height, width), "own", [like((cells, channels), F32)] * 2)(
        after(counts, (side, w_other)), feat, row, col
    )
    h0 = call(functools.partial(finish_kernel, height, width), "finish", [like((cells, channels), BF16)])(
        scalars, numer, denom, from_first, from_second
    )[0]
    h0_first, h0_second = with_partners(h0, h0)
    side_got = swap(side, "dp", outer)
    lower = member % 2 == 0
    w_two = jnp.concatenate([jnp.where(lower, w_second, w_other), jnp.where(lower, w_other, w_second)], axis=0)
    w_two = after(w_two, h0)
    chunk = math.gcd(w_two.shape[0], hidden)
    wide_cells = (height + 2) * width
    partial_outs = [like((cells, hidden), F32), like((cells, hidden), BF16)]
    back, back_other, stack = call(
        functools.partial(back_kernel, height, width, chunk),
        "back",
        partial_outs + [like((4, cells, hidden), BF16)],
        scratch=[pltpu.VMEM((2, 3, wide_cells, hidden), BF16)],
    )(after(scalars, h0), cot, cot_got, side, side_got, w_two)
    back_got = swap(back_other, "dp", outer)

    w_near = jnp.stack([w_first, after(w_got, h0)])
    w_far = swap(w_near, "dp", 1)
    pre1, h1, edge, h0_near = call(
        functools.partial(first_kernel, height, width, distances([outer, 1])),
        "first",
        [
            like((cells, hidden), F32),
            like((cells, hidden), BF16),
            side,
            like((width, (height + 2) * channels), BF16),
        ],
        scratch=[pltpu.VMEM((n_dp * w_first.shape[0], hidden), BF16)],
    )(after(scalars, back), h0, h0_first, h0_second, w_near, w_far)

    h1_got = swap(h1, "dp", outer)
    h1_far, h1_far_got, stack_far = [swap(v, "dp", 1) for v in (h1, h1_got, stack)]

    rows_two, rows_one = w_second.shape[0], w_first.shape[0]
    part = hidden // n_lat
    turned = call(
        functools.partial(turn_kernel, height, width, rows_two),
        "turn",
        [like((3, hidden, n_dp * cells), BF16)],
        scratch=[pltpu.VMEM((n_dp, wide_cells, hidden), BF16)],
    )(after(scalars, (h1, back_got)), stack, stack_far)[0]
    piece = like((n_lat // 2, part // 2, rows_two), BF16)
    keep_one, send_one, keep_two, send_two = call(
        functools.partial(grad_second_kernel, rows_two, 3, n_lat),
        "gradsecond",
        [piece] * 4,
        scratch=[pltpu.VMEM((hidden, 3 * hidden), F32)],
    )(scalars, turned, h1, h1_got, h1_far, h1_far_got)
    sent = call(dpre_kernel, "dpre", [like((hidden + (height + 2) // height * width, cells), BF16)])(
        after(scalars, keep_one), pre1, cot, h0_near, back, back_got
    )[0]
    streams = [(keep_one, swap(send_one, "lat", 1)), (keep_two, swap(send_two, "lat", 2))]
    offsets = [[k for k in range(n_lat) if not k & bit] for bit in (1, 2)]
    ((stay_one, go_one), (stay_two, go_two)), _ = add_step(streams, offsets, (2, 1))
    got_one, got_two = swap(go_one, "lat", 2), swap(go_two, "lat", 1)
    stay, go = call(meet_kernel, "meet", [like((n_lat // 8, part, rows_two), BF16)] * 2, scalars=0)(
        stay_one, got_one, stay_two, got_two
    )
    grad_second = finished(stay, swap(go, "lat", 4), list(range(0, n_lat, 8)), lat_bits[3:])

    keep, send = call(
        functools.partial(grad_first_kernel, height, width, rows_one, n_lat, outer),
        "gradfirst",
        [like((n_lat, part, rows_one), BF16)] * 2,
        scratch=[pltpu.VMEM((2, wide_cells, channels), BF16)],
    )(scalars, sent, swap(sent, "dp", 1))
    first_got = swap(send, "dp", outer)
    grad_first = finished(after(keep, streams), first_got, list(range(n_lat)), lat_bits)

    edge_got = swap(after(edge, send), "dp", outer)
    second, second_other = call(
        functools.partial(second_kernel, height, width, chunk),
        "second",
        partial_outs,
        scratch=[pltpu.VMEM((2, 3, hidden // chunk, wide_cells, chunk), BF16)],
    )(after(scalars, first_got), h1, h1_got, edge, edge_got, w_two)
    encoded = (second + swap(second_other, "dp", outer).astype(F32)).astype(BF16).reshape(1, height, width, hidden)
    return encoded, grad_first, grad_second


def with_halo(value, sides, width):
    for axis, dim in sides:
        size, length = (lax.axis_size(axis), value.shape[dim])
        up = [(i, (i + 1) % size) for i in range(size - 1)]
        down = [(j, i) for i, j in up]
        last = lax.slice_in_dim(value, length - width, length, axis=dim)
        first = lax.slice_in_dim(value, 0, width, axis=dim)
        before = lax.ppermute(last, axis, up)
        after = lax.ppermute(first, axis, down)
        value = jnp.concatenate([before, value, after], axis=dim)
    return value


def passed_along(block, axis, distance):
    devices = range(lax.axis_size(axis))
    route = [(i - distance, i) for i in devices if i - distance in devices]
    return lax.ppermute(block, axis, route)


def gauss_weights(cell_rows, cell_cols, rows, cols, valid):
    drow = cell_rows[:, None] - rows[None, :]
    dcol = cell_cols[:, None] - cols[None, :]
    return valid[None, :] * jnp.exp(-0.5 * (drow * drow + dcol * dcol))


def haloed_rows(grid):
    padded = with_halo(grid, (("lat", 0),), 1)
    return jnp.pad(padded, ((0, 0), (1, 1), (0, 0)))


def padded_patches(padded, height, width):
    pieces = [padded[dy : dy + height, dx : dx + width] for dy in range(3) for dx in range(3)]
    return jnp.concatenate(pieces, axis=-1).reshape(height * width, -1)


def plain(obs_feat, obs_row, obs_col, counts, edge_index, edge_mask, cotangent, w_first, w_second):
    feat = obs_feat[0]
    slot_total = feat.shape[0]
    channels = feat.shape[1]
    height = cotangent.shape[1]
    width = cotangent.shape[2]
    hidden = cotangent.shape[3]
    band_index = lax.axis_index("lat")
    band_base = (band_index * height).astype(jnp.float32)
    count = counts[0, 0]
    row_g = obs_row[0] + band_base
    col_b = obs_col[0]
    slots = jnp.arange(slot_total, dtype=jnp.int32)
    valid = (slots < count).astype(jnp.float32)

    def pick(listed, listed_mask):
        picked_feat = jnp.take(feat, listed, axis=0)
        live_flag = listed_mask.astype(jnp.float32) * (listed < count).astype(jnp.float32)
        place = jnp.stack([jnp.take(row_g, listed), jnp.take(col_b, listed), live_flag], axis=1)
        return (picked_feat, place)

    low_feat, low_place = pick(edge_index[0, 0, 0], edge_mask[0, 0, 0])
    high_feat, high_place = pick(edge_index[0, 0, 1], edge_mask[0, 0, 1])
    below_feat, below_place = passed_along((high_feat, high_place), "lat", 1)
    above_feat, above_place = passed_along((low_feat, low_place), "lat", -1)
    recv_feat = jnp.concatenate([below_feat, above_feat], 0)
    recv_place = jnp.concatenate([below_place, above_place], 0)
    cells = jnp.arange(height * width, dtype=jnp.int32)
    cell_rows = band_base + (cells // width).astype(jnp.float32)
    cell_cols = (cells % width).astype(jnp.float32)
    edge_weights = gauss_weights(
        cell_rows, cell_cols, recv_place[:, 0], recv_place[:, 1], recv_place[:, 2]
    )
    numer = jnp.dot(edge_weights, recv_feat, precision=lax.Precision.HIGHEST)
    denom = jnp.sum(edge_weights, 1)
    own_weights = gauss_weights(cell_rows, cell_cols, row_g, col_b, valid)
    numer = numer + jnp.dot(own_weights, feat, precision=lax.Precision.HIGHEST)
    denom = denom + jnp.sum(own_weights, 1)
    h0 = (
        (numer / jnp.sqrt(1.0 + denom)[:, None])
        .astype(jnp.bfloat16)
        .reshape(height, width, channels)
    )

    def fold_rows(patches, piece):
        return jnp.dot(patches, piece, preferred_element_type=jnp.float32)

    patches0 = padded_patches(haloed_rows(h0), height, width)
    pre1 = fold_rows(patches0, lax.all_gather(w_first, "dp", axis=0, tiled=True))
    h1 = jax.nn.silu(pre1).astype(jnp.bfloat16)
    patches1 = padded_patches(haloed_rows(h1.reshape(height, width, hidden)), height, width)
    pre2 = fold_rows(patches1, lax.all_gather(w_second, "dp", axis=0, tiled=True))
    encoded = (h1.astype(jnp.float32) + pre2).astype(jnp.bfloat16).reshape(1, height, width, hidden)
    cot = cotangent[0]
    cot_pad = haloed_rows(cot).reshape(-1, hidden)
    spread = lax.dot_general(
        cot_pad,
        lax.all_gather(w_second, "dp", axis=0, tiled=True),
        (((1,), (1,)), ((), ())),
        preferred_element_type=jnp.float32,
    )
    spread = spread.reshape(height + 2, width + 2, 9, hidden)
    dh1 = cot.astype(jnp.float32)
    for dy in range(3):
        for dx in range(3):
            dh1 = dh1 + spread[2 - dy : 2 - dy + height, 2 - dx : 2 - dx + width, dy * 3 + dx]
    sig = jax.nn.sigmoid(pre1)
    dpre1 = (dh1.reshape(-1, hidden) * sig * (1.0 + pre1 * (1.0 - sig))).astype(jnp.bfloat16)
    cot_flat = cot.reshape(-1, hidden)
    contract = (((0,), (0,)), ((), ()))
    grad_two = lax.dot_general(patches1, cot_flat, contract, preferred_element_type=jnp.float32)
    grad_one = lax.dot_general(patches0, dpre1, contract, preferred_element_type=jnp.float32)
    partial_one, partial_two = (
        lax.psum_scatter(
            grad_one.astype(jnp.bfloat16), "dp", scatter_dimension=0, tiled=True
        ).astype(jnp.float32),
        lax.psum_scatter(
            grad_two.astype(jnp.bfloat16), "dp", scatter_dimension=0, tiled=True
        ).astype(jnp.float32),
    )
    grad_first, grad_second = (
        lax.psum_scatter(
            partial_one.astype(jnp.bfloat16), "lat", scatter_dimension=1, tiled=True
        ).astype(jnp.float32),
        lax.psum_scatter(
            partial_two.astype(jnp.bfloat16), "lat", scatter_dimension=1, tiled=True
        ).astype(jnp.float32),
    )
    return (encoded, grad_first, grad_second)


def fits(mesh, height, width, hidden, channels, rows_one, rows_two):
    n_dp, n_lat = mesh.shape["dp"], mesh.shape["lat"]
    powers = all(n & (n - 1) == 0 for n in (n_dp, n_lat, hidden, channels))
    grid = height == 2 and width == channels and width % 128 == 0 and (height + 2) * channels == hidden
    blocks = all(
        [(d * rows + rows - 1) // size - d * rows // size for d in range(n_dp)] == [2] * n_dp
        for rows, size in ((rows_one, channels), (rows_two, hidden))
    )
    return powers and grid and n_dp == 2 * 2 and n_lat > 4 and (hidden // n_lat) % 32 == 0 and blocks and rows_one % 32 == 0 and rows_two % 128 == 0


def solution(mesh):
    in_specs = (
        P("dp", "lat", None),
        P("dp", "lat"),
        P("dp", "lat"),
        P("dp", "lat"),
        P("dp", "lat", None, None),
        P("dp", "lat", None, None),
        P("dp", "lat", None, None),
        P("dp", None),
        P("dp", None),
    )
    out_specs = (P("dp", "lat", None, None), P("dp", "lat"), P("dp", "lat"))

    def run(*args):
        feat, cot, w_first, w_second = args[0], args[6], args[7], args[8]
        n_dp, n_lat = mesh.shape["dp"], mesh.shape["lat"]
        shapes = (cot.shape[1] // n_lat, *cot.shape[2:], feat.shape[2], w_first.shape[0] // n_dp, w_second.shape[0] // n_dp)
        step = local if fits(mesh, *shapes) else plain
        return jax.shard_map(step, mesh=mesh, in_specs=in_specs, out_specs=out_specs, check_vma=False)(*args)

    return run
```

```python
import functools
import math

import jax
import jax.numpy as jnp
from jax import lax
from jax.experimental import pallas as pl
from jax.experimental.pallas import tpu as pltpu
from jax.sharding import PartitionSpec as P

BF16 = jnp.bfloat16
F32 = jnp.float32
VMEM = pl.BlockSpec(memory_space=pltpu.VMEM)
SMEM = pl.BlockSpec(memory_space=pltpu.SMEM)
FAR = pl.BlockSpec(memory_space=pltpu.HBM)


def call(kernel, name, outs, scratch=(), scalars=1, far=0, grant=48):
    def run(*args):
        return pl.pallas_call(
            kernel,
            name=name,
            out_shape=outs,
            in_specs=[SMEM] * scalars + [VMEM] * (len(args) - scalars - far) + [FAR] * far,
            out_specs=[VMEM] * len(outs),
            scratch_shapes=list(scratch),
            cost_estimate=pl.CostEstimate(flops=COST[name], bytes_accessed=0, transcendentals=0),
            compiler_params=pltpu.CompilerParams(vmem_limit_bytes=grant * 2**20),
        )(*args)

    return run


COST = {"edges": 4107269028, "own": 657163044, "finish": 1150035328, "back": 4600141312, "first": 24202651983, "turn": 2957233700, "gradsecond": 4107269028, "dpre": 1314326089, "gradfirst": 2464361417, "second": 4435850551, "add": 1150035328, "meet": 1150035328, "last": 1150035328}


def like(shape, dtype):
    return jax.ShapeDtypeStruct(shape, dtype)


def dot(a, b):
    return jnp.dot(a, b, preferred_element_type=F32)


def dot_nt(a, b):
    return lax.dot_general(a, b, (((1,), (1,)), ((), ())), preferred_element_type=F32)


def shifted(x, step, width):
    if isinstance(step, int) and step == 0:
        return x
    total = x.shape[0]
    wide = pltpu.roll(x.astype(F32), lax.rem(total - step, total) if not isinstance(step, int) else (total - step) % total, 0)
    place = lax.broadcasted_iota(jnp.int32, x.shape, 0) % width + step
    return jnp.where((place >= 0) & (place < width), wide, 0.0).astype(x.dtype)


def column_factor(col_ref, width):
    cells = lax.broadcasted_iota(jnp.int32, (width, col_ref.shape[1]), 0).astype(F32)
    away = cells - col_ref[...]
    return jnp.exp(-0.5 * (away * away))


def cell_weights(factor, row_ref, rows):
    parts = []
    for row in rows:
        away = row - row_ref[...]
        parts.append((factor * jnp.exp(-0.5 * (away * away))).astype(BF16))
    return jnp.concatenate(parts, axis=0)


def edge_kernel(height, width, s_ref, *refs):
    far, (first_ref, second_ref), near, sems = refs[:6], refs[6:8], refs[8:14], refs[14]
    copies = [pltpu.make_async_copy(a, b, sems.at[n]) for n, (a, b) in enumerate(zip(far, near))]
    for copy in copies:
        copy.start()
    for copy in copies:
        copy.wait()
    feat_ref, row_ref, col_ref, index_ref, mask_ref, cot_ref = near
    up = lax.rem(lax.axis_index("lat"), 2) == 0
    low, high = cot_ref[:width], cot_ref[(height - 1) * width :]
    lanes = feat_ref.shape[1]
    for out_ref, side in ((first_ref, jnp.where(up, high, low)), (second_ref, jnp.where(up, low, high))):
        for q in range(side.shape[1] // lanes):
            at = height * (width + 16) + q * width
            out_ref[at : at + width] = side[:, q * lanes : (q + 1) * lanes]
    slots, channels = feat_ref.shape
    factor = column_factor(col_ref, width)
    entries = index_ref.shape[1]
    slot = lax.broadcasted_iota(jnp.int32, (slots, entries), 0)
    live = slot < s_ref[0, 0]
    feat = feat_ref[...]
    totals = []
    for side in range(2):
        named = jnp.where((slot == index_ref[side : side + 1]) & live, mask_ref[side : side + 1], 0)
        times = jnp.sum(named.astype(F32), axis=1, keepdims=True)
        values = jnp.concatenate([feat * times, jnp.broadcast_to(times, feat.shape)], axis=1)
        offset = height if side == 1 else -height
        weights = cell_weights(factor, row_ref, [float(offset + i) for i in range(height)])
        totals.append(dot(weights, values.astype(BF16)))
    for out_ref, one, other in ((first_ref, 1, 0), (second_ref, 0, 1)):
        total = jnp.where(up, totals[one], totals[other])
        out_ref[: height * width] = total[:, :channels].astype(BF16)
        for i in range(height):
            turned = total[i * width : (i + 1) * width, channels:].T[:16]
            out_ref[height * width + 16 * i : height * width + 16 * (i + 1)] = turned.astype(BF16)


def own_kernel(height, width, s_ref, feat_ref, row_ref, col_ref, numer_ref, denom_ref):
    slots, channels = feat_ref.shape
    live = lax.broadcasted_iota(jnp.int32, (slots, channels), 0) < s_ref[0, 0]
    values = jnp.concatenate([jnp.where(live, feat_ref[...], 0.0), live.astype(F32)], axis=1)
    weights = cell_weights(column_factor(col_ref, width), row_ref, [float(i) for i in range(height)])
    total = dot(weights, values.astype(BF16))
    numer_ref[...] = total[:, :channels]
    denom_ref[...] = total[:, channels:]


def partners(s_ref):
    first = jnp.where(s_ref[2] == 1, s_ref[4], s_ref[3])
    second = jnp.where(s_ref[2] == 1, s_ref[3], s_ref[4])
    return first, second


def finish_kernel(height, width, s_ref, numer_ref, denom_ref, first_ref, second_ref, out_ref, side_ref):
    first, second = partners(s_ref)
    cells = height * width

    def got(part):
        return jnp.where(first == 1, first_ref[part].astype(F32), 0.0) + jnp.where(
            second == 1, second_ref[part].astype(F32), 0.0
        )

    for i in range(height):
        rows = slice(i * width, (i + 1) * width)
        added = got(slice(cells + 16 * i, cells + 16 * i + 16))[:1]
        added = jnp.broadcast_to(added, (width, width)).T[:, : numer_ref.shape[1]]
        numer = numer_ref[rows] + got(rows)
        out_ref[rows] = (numer * lax.rsqrt(1.0 + denom_ref[rows] + added)).astype(BF16)
    lanes = numer_ref.shape[1]
    for n, ref in enumerate((first_ref, second_ref)):
        for q in range(side_ref.shape[1] // lanes):
            at = height * (width + 16) + q * width
            side_ref[n * width : (n + 1) * width, q * lanes : (q + 1) * lanes] = ref[at : at + width]


def side_rows(s_ref, first, second):
    up = s_ref[2] == 1
    none = jnp.zeros_like(first)
    below = jnp.where(s_ref[3] == 1, jnp.where(up, second, first), none)
    above = jnp.where(s_ref[4] == 1, jnp.where(up, first, second), none)
    return below, above


def first_kernel(height, width, offsets, s_ref, own_ref, a_ref, b_ref, w_near, w_far, *refs):
    pre_ref, h1_ref, edge_ref, near_ref, w_full = refs
    channels = own_ref.shape[1]
    count, piece, hidden = w_near.shape
    for place, offset in enumerate(offsets):
        at = lax.bitwise_xor(s_ref[5], offset) * piece
        w_full[pl.ds(pl.multiple_of(at, 32), piece)] = (w_near, w_far)[place // count][place % count]
    below, above = side_rows(s_ref, a_ref[...], b_ref[...])
    grid = jnp.concatenate([below[-2 * width :], own_ref[...], above[: 2 * width]], axis=0)
    rows = height + 2
    moved = [shifted(grid, step, width) for step in (-1, 0, 1)]
    patches = jnp.concatenate([moved[dx][dy * width : (dy + rows) * width] for dy in range(3) for dx in range(3)], axis=1)
    pre = dot(patches, w_full[...])
    h1 = (pre * jax.nn.sigmoid(pre)).astype(BF16)
    zero = jnp.zeros((width, hidden), BF16)
    pre_ref[...] = pre[width:-width]
    h1_ref[...] = h1[width:-width]
    edge_ref[:width] = jnp.where(s_ref[3] == 1, h1[:width], zero)
    edge_ref[width:] = jnp.where(s_ref[4] == 1, h1[-width:], zero)
    near = grid[width:-width]
    for i in range(rows):
        near_ref[:, i * channels : (i + 1) * channels] = near[i * width : (i + 1) * width]


def wide_rows(s_ref, width, cot_ref, side_ref):
    below, above = side_rows(s_ref, side_ref[:width], side_ref[width:])
    return jnp.concatenate([below, cot_ref[...], above], axis=0)


def chunk_place(s_ref, step, per_group, per_block):
    chunk = s_ref[6] * per_group + step
    block = chunk // per_block
    return block // 3, block % 3, chunk % per_block


def back_kernel(height, width, chunk, s_ref, cot_ref, cot_got, side_ref, side_got, w_ref, own_ref, other_ref, stack_ref, moved_ref):
    hidden = w_ref.shape[1]
    halves = hidden // chunk
    cells = height * width
    per_group = w_ref.shape[0] // chunk
    for place, ref in enumerate((cot_ref, cot_got, side_ref, side_got)):
        stack_ref[place] = ref[...]
    for member, out_ref in enumerate((own_ref, other_ref)):
        grid = wide_rows(s_ref, width, (cot_ref, cot_got)[member], (side_ref, side_got)[member])
        for dx in range(3):
            moved_ref[member, dx] = shifted(grid, 1 - dx, width)
        totals = [jnp.zeros((cells, chunk), F32) for _ in range(halves)]
        for step in range(per_group):
            dy, dx, _ = chunk_place(s_ref, step, per_group, halves)
            rows = pl.ds(pl.multiple_of((2 - dy) * width, width), cells)
            totals[step % halves] += dot_nt(moved_ref[member, dx, rows], w_ref[step * chunk : (step + 1) * chunk])
        start = chunk_place(s_ref, 0, per_group, halves)[2]
        for rank in range(halves):
            half = lax.rem(start + rank, halves)
            columns = pl.ds(pl.multiple_of(half * chunk, chunk), chunk)
            out_ref[:, columns] = totals[rank].astype(out_ref.dtype)


def second_kernel(height, width, chunk, s_ref, mid_one, mid_two, edge_one, edge_two, w_ref, own_ref, other_ref, moved_ref):
    hidden = w_ref.shape[1]
    halves = hidden // chunk
    cells = height * width
    per_group = w_ref.shape[0] // chunk
    for member, (mid_ref, edge_ref, out_ref) in enumerate(((mid_one, edge_one, own_ref), (mid_two, edge_two, other_ref))):
        grid = jnp.concatenate([edge_ref[:width], mid_ref[...], edge_ref[width:]], axis=0)
        for dx in range(3):
            place = shifted(grid, dx - 1, width)
            for half in range(halves):
                moved_ref[member, dx, half] = place[:, half * chunk : (half + 1) * chunk]
        total = mid_ref[...].astype(F32) if member == 0 else jnp.zeros((cells, hidden), F32)
        for step in range(per_group):
            dy, dx, half = chunk_place(s_ref, step, per_group, halves)
            rows = pl.ds(pl.multiple_of(dy * width, width), cells)
            total += dot(moved_ref[member, dx, half, rows], w_ref[step * chunk : (step + 1) * chunk])
        out_ref[...] = total.astype(out_ref.dtype)


def dpre_kernel(s_ref, pre_ref, cot_ref, near_ref, own_ref, got_ref, out_ref):
    pre = pre_ref[...]
    back = cot_ref[...].astype(F32) + own_ref[...] + got_ref[...].astype(F32)
    sig = jax.nn.sigmoid(pre)
    hidden, cells = pre.shape[1], pre.shape[0]
    out_ref[:hidden] = (back * sig * (1.0 + pre * (1.0 - sig))).T.astype(BF16)
    width = near_ref.shape[0]
    for half in range(near_ref.shape[1] // cells):
        out_ref[hidden + half * width : hidden + (half + 1) * width] = near_ref[:, half * cells : (half + 1) * cells]


def turn_kernel(height, width, rows_out, s_ref, *refs):
    near_ref, far_ref, out_ref, wide_ref = refs
    times, count = wide_ref.shape[0], wide_ref.shape[0] // 2
    _, cells, hidden = near_ref.shape
    first = (s_ref[5] * rows_out) // hidden
    for t in range(times):
        ref = (near_ref, far_ref)[t // count]
        wide_ref[t] = wide_rows(s_ref, width, ref.at[t % count], ref.at[count + t % count])
    for dx in range(3):
        j = lax.rem(dx + 3 - lax.rem(first, 3), 3)
        dy = jnp.minimum(first + j, 8) // 3
        rows = pl.ds(pl.multiple_of((2 - dy) * width, width), cells)
        for t in range(times):
            x = shifted(wide_ref[t, rows], 1 - dx, width)
            out_ref[j, :, t * cells : (t + 1) * cells] = x.astype(F32).T.astype(BF16)


def grad_second_kernel(rows_out, blocks, lats, s_ref, turned_ref, *refs):
    h1_refs, (keep_one, send_one, keep_two, send_two, full_ref) = refs[:-5], refs[-5:]
    hidden = h1_refs[0].shape[1]
    base = s_ref[5] * rows_out
    off = base - (base // hidden) * hidden
    h1 = jnp.concatenate([h1_ref[...] for h1_ref in h1_refs], axis=0)
    for j in range(blocks):
        full_ref[:, j * hidden : (j + 1) * hidden] = dot(turned_ref[j], h1)
    part = hidden // lats
    half = part // 2
    columns = pl.ds(pl.multiple_of(off, 128), rows_out)
    slots = [0] * 4
    for k in range(lats):
        at = lax.bitwise_xor(s_ref[0], k) * part
        for number, (keep_ref, send_ref, bit) in enumerate(((keep_one, send_one, 1), (keep_two, send_two, 2))):
            sent = 1 if k & bit else 0
            place = 2 * number + sent
            rows = pl.ds(pl.multiple_of(at + number * half, half), half)
            (keep_ref, send_ref)[sent][slots[place]] = full_ref[rows, columns].astype(BF16)
            slots[place] += 1


def grad_first_kernel(height, width, rows_out, lats, distance, s_ref, *refs):
    sent_refs, (keep_ref, send_ref, full_ref) = refs[:-3], refs[-3:]
    cells = sent_refs[0].shape[1]
    channels = full_ref.shape[2]
    rows = height + 2
    hidden = rows * channels
    wide = 3 * channels
    part = hidden // lats
    for t, sent_ref in enumerate(sent_refs):
        for i in range(rows):
            half, side = i // height, i % height
            full_ref[t, i * width : (i + 1) * width] = sent_ref[
                hidden + half * width : hidden + (half + 1) * width, side * channels : (side + 1) * channels
            ]
    for out_ref, away in ((send_ref, distance), (keep_ref, 0)):
        base = lax.bitwise_xor(s_ref[5], away) * rows_out
        first = base // channels
        off = base - first * channels
        turn = lax.rem(first, 3)
        total = jnp.zeros((hidden, wide), F32)
        for t, sent_ref in enumerate(sent_refs):
            pieces = []
            for dx in range(3):
                dy = jnp.minimum(first + lax.rem(dx + 3 - turn, 3), 8) // 3
                near = full_ref[t, pl.ds(pl.multiple_of(dy * width, width), cells)]
                pieces.append(shifted(near, dx - 1, width))
            total += dot(sent_ref[:hidden], jnp.concatenate(pieces, axis=1))
        total = pltpu.roll(total, lax.rem(2 * wide - off - turn * channels, wide), 1)[:, :rows_out].astype(BF16)
        for k in range(lats):
            out_ref[lax.bitwise_xor(s_ref[0], k)] = total[k * part : (k + 1) * part]


def add_kernel(places, *refs):
    count = len(places)
    for n, (stay, go) in enumerate(places):
        keep_ref, got_ref = refs[2 * n : 2 * n + 2]
        stay_ref, go_ref = refs[2 * (count + n) : 2 * (count + n) + 2]
        for out_ref, picked in ((stay_ref, stay), (go_ref, go)):
            for slot, place in enumerate(picked):
                out_ref[slot] = (keep_ref[place].astype(F32) + got_ref[place].astype(F32)).astype(BF16)


def meet_kernel(one_ref, got_one, two_ref, got_two, stay_ref, go_ref):
    half = one_ref.shape[1]
    for rows, keep_ref, got_ref in ((slice(0, half), one_ref, got_one), (slice(half, 2 * half), two_ref, got_two)):
        for place in range(keep_ref.shape[0]):
            out_ref = (stay_ref, go_ref)[place % 2]
            out_ref[place // 2, rows] = (keep_ref[place].astype(F32) + got_ref[place].astype(F32)).astype(BF16)


def last_kernel(keep_ref, got_ref, out_ref):
    out_ref[...] = keep_ref[0].astype(F32) + got_ref[0].astype(F32)


def swap(value, axis, bit):
    return lax.ppermute(value, axis, [(i, i ^ bit) for i in range(lax.axis_size(axis))])


def after(value, other):
    return lax.optimization_barrier((value, other))[0]


def distances(bits):
    order = [0]
    for bit in bits:
        order = order + [n ^ bit for n in order]
    return order


def with_partners(first, second):
    size = lax.axis_size("lat")
    pairs = [(i, i + 1) for i in range(1, size - 1, 2)]
    pairs = pairs + [(j, i) for i, j in pairs] + [(0, 0), (size - 1, size - 1)]
    return swap(first, "lat", 1), lax.ppermute(second, "lat", pairs)


def parted(offsets, bit):
    stay = [n for n, k in enumerate(offsets) if not k & bit]
    go = [n for n, k in enumerate(offsets) if k & bit]
    return (stay, go), [offsets[n] for n in stay]


def add_step(streams, offsets, bits):
    places, left = zip(*[parted(o, b) for o, b in zip(offsets, bits)])
    outs = [like((len(side), *keep.shape[1:]), BF16) for (keep, _), place in zip(streams, places) for side in place]
    flat = call(functools.partial(add_kernel, places), "add", outs, scalars=0)(*[v for pair in streams for v in pair])
    return [flat[n : n + 2] for n in range(0, len(flat), 2)], list(left)


def finished(stay, got, offsets, bits):
    for bit in bits:
        ((stay, go),), (offsets,) = add_step([(stay, got)], [offsets], [bit])
        got = swap(go, "lat", bit)
    return call(last_kernel, "last", [like(stay.shape[1:], F32)], scalars=0)(stay, got)[0].T


def local(obs_feat, obs_row, obs_col, counts, edge_index, edge_mask, cotangent, w_first, w_second):
    _, height, width, hidden = cotangent.shape
    channels = obs_feat.shape[2]
    cells = height * width
    n_dp, n_lat = lax.axis_size("dp"), lax.axis_size("lat")
    band, member = lax.axis_index("lat"), lax.axis_index("dp")
    scalars = jnp.stack(
        [
            band,
            counts[0, 0],
            1 - band % 2,
            (band > 0).astype(jnp.int32),
            (band < n_lat - 1).astype(jnp.int32),
            member,
            member // 2,
        ]
    ).astype(jnp.int32)
    lat_bits = [1 << n for n in range(n_lat.bit_length() - 1)]
    outer = n_dp // 2
    cot = cotangent[0].reshape(cells, hidden)

    feat, row, col = obs_feat[0], obs_row, obs_col
    payload = like((height * (width + 16) + width * hidden // channels, channels), BF16)
    observed = [feat, row, col, edge_index[0, 0], edge_mask[0, 0], cot]
    edges = call(
        functools.partial(edge_kernel, height, width),
        "edges",
        [payload, payload],
        scratch=[pltpu.VMEM(v.shape, v.dtype) for v in observed] + [pltpu.SemaphoreType.DMA((len(observed),))],
        far=len(observed),
        grant=60,
    )(counts, *observed)
    cot_got, w_got, w_other = swap(cot, "dp", outer), swap(w_first, "dp", outer), swap(w_second, "dp", 1)
    from_first, from_second = with_partners(*edges)
    numer, denom = call(functools.partial(own_kernel, height, width), "own", [like((cells, channels), F32)] * 2)(
        after(counts, w_other), feat, row, col
    )
    sides_out = like((2 * width, hidden), BF16)
    h0, side = call(functools.partial(finish_kernel, height, width), "finish", [like((cells, channels), BF16), sides_out])(
        scalars, numer, denom, from_first, from_second
    )
    h0_first, h0_second = with_partners(h0, h0)
    side_got = swap(side, "dp", outer)
    lower = member % 2 == 0
    w_two = jnp.concatenate([jnp.where(lower, w_second, w_other), jnp.where(lower, w_other, w_second)], axis=0)
    w_two = after(w_two, h0)
    chunk = math.gcd(w_two.shape[0], hidden)
    wide_cells = (height + 2) * width
    partial_outs = [like((cells, hidden), F32), like((cells, hidden), BF16)]
    back, back_other, stack = call(
        functools.partial(back_kernel, height, width, chunk),
        "back",
        partial_outs + [like((4, cells, hidden), BF16)],
        scratch=[pltpu.VMEM((2, 3, wide_cells, hidden), BF16)],
    )(after(scalars, h0), cot, cot_got, side, side_got, w_two)
    back_got = swap(back_other, "dp", outer)

    w_near = jnp.stack([w_first, after(w_got, h0)])
    w_far = swap(w_near, "dp", 1)
    pre1, h1, edge, h0_near = call(
        functools.partial(first_kernel, height, width, distances([outer, 1])),
        "first",
        [
            like((cells, hidden), F32),
            like((cells, hidden), BF16),
            sides_out,
            like((width, (height + 2) * channels), BF16),
        ],
        scratch=[pltpu.VMEM((n_dp * w_first.shape[0], hidden), BF16)],
    )(after(scalars, back), h0, h0_first, h0_second, w_near, w_far)

    h1_got = swap(h1, "dp", outer)
    h1_far, h1_far_got, stack_far = [swap(v, "dp", 1) for v in (h1, h1_got, stack)]

    rows_two, rows_one = w_second.shape[0], w_first.shape[0]
    part = hidden // n_lat
    turned = call(
        functools.partial(turn_kernel, height, width, rows_two),
        "turn",
        [like((3, hidden, n_dp * cells), BF16)],
        scratch=[pltpu.VMEM((n_dp, wide_cells, hidden), BF16)],
    )(after(scalars, (h1, back_got)), stack, stack_far)[0]
    piece = like((n_lat // 2, part // 2, rows_two), BF16)
    keep_one, send_one, keep_two, send_two = call(
        functools.partial(grad_second_kernel, rows_two, 3, n_lat),
        "gradsecond",
        [piece] * 4,
        scratch=[pltpu.VMEM((hidden, 3 * hidden), F32)],
    )(scalars, turned, h1, h1_got, h1_far, h1_far_got)
    sent = call(dpre_kernel, "dpre", [like((hidden + (height + 2) // height * width, cells), BF16)])(
        after(scalars, keep_one), pre1, cot, h0_near, back, back_got
    )[0]
    streams = [(keep_one, swap(send_one, "lat", 1)), (keep_two, swap(send_two, "lat", 2))]
    offsets = [[k for k in range(n_lat) if not k & bit] for bit in (1, 2)]
    ((stay_one, go_one), (stay_two, go_two)), _ = add_step(streams, offsets, (2, 1))
    got_one, got_two = swap(go_one, "lat", 2), swap(go_two, "lat", 1)
    stay, go = call(meet_kernel, "meet", [like((n_lat // 8, part, rows_two), BF16)] * 2, scalars=0)(
        stay_one, got_one, stay_two, got_two
    )
    grad_second = finished(stay, swap(go, "lat", 4), list(range(0, n_lat, 8)), lat_bits[3:])

    keep, send = call(
        functools.partial(grad_first_kernel, height, width, rows_one, n_lat, outer),
        "gradfirst",
        [like((n_lat, part, rows_one), BF16)] * 2,
        scratch=[pltpu.VMEM((2, wide_cells, channels), BF16)],
    )(scalars, sent, swap(sent, "dp", 1))
    first_got = swap(send, "dp", outer)
    grad_first = finished(after(keep, streams), first_got, list(range(n_lat)), lat_bits)

    edge_got = swap(after(edge, send), "dp", outer)
    second, second_other = call(
        functools.partial(second_kernel, height, width, chunk),
        "second",
        partial_outs,
        scratch=[pltpu.VMEM((2, 3, hidden // chunk, wide_cells, chunk), BF16)],
    )(after(scalars, first_got), h1, h1_got, edge, edge_got, w_two)
    encoded = (second + swap(second_other, "dp", outer).astype(F32)).astype(BF16).reshape(1, height, width, hidden)
    return encoded, grad_first, grad_second


def with_halo(value, sides, width):
    for axis, dim in sides:
        size, length = (lax.axis_size(axis), value.shape[dim])
        up = [(i, (i + 1) % size) for i in range(size - 1)]
        down = [(j, i) for i, j in up]
        last = lax.slice_in_dim(value, length - width, length, axis=dim)
        first = lax.slice_in_dim(value, 0, width, axis=dim)
        before = lax.ppermute(last, axis, up)
        after = lax.ppermute(first, axis, down)
        value = jnp.concatenate([before, value, after], axis=dim)
    return value


def passed_along(block, axis, distance):
    devices = range(lax.axis_size(axis))
    route = [(i - distance, i) for i in devices if i - distance in devices]
    return lax.ppermute(block, axis, route)


def gauss_weights(cell_rows, cell_cols, rows, cols, valid):
    drow = cell_rows[:, None] - rows[None, :]
    dcol = cell_cols[:, None] - cols[None, :]
    return valid[None, :] * jnp.exp(-0.5 * (drow * drow + dcol * dcol))


def haloed_rows(grid):
    padded = with_halo(grid, (("lat", 0),), 1)
    return jnp.pad(padded, ((0, 0), (1, 1), (0, 0)))


def padded_patches(padded, height, width):
    pieces = [padded[dy : dy + height, dx : dx + width] for dy in range(3) for dx in range(3)]
    return jnp.concatenate(pieces, axis=-1).reshape(height * width, -1)


def plain(obs_feat, obs_row, obs_col, counts, edge_index, edge_mask, cotangent, w_first, w_second):
    feat = obs_feat[0]
    slot_total = feat.shape[0]
    channels = feat.shape[1]
    height = cotangent.shape[1]
    width = cotangent.shape[2]
    hidden = cotangent.shape[3]
    band_index = lax.axis_index("lat")
    band_base = (band_index * height).astype(jnp.float32)
    count = counts[0, 0]
    row_g = obs_row[0] + band_base
    col_b = obs_col[0]
    slots = jnp.arange(slot_total, dtype=jnp.int32)
    valid = (slots < count).astype(jnp.float32)

    def pick(listed, listed_mask):
        picked_feat = jnp.take(feat, listed, axis=0)
        live_flag = listed_mask.astype(jnp.float32) * (listed < count).astype(jnp.float32)
        place = jnp.stack([jnp.take(row_g, listed), jnp.take(col_b, listed), live_flag], axis=1)
        return (picked_feat, place)

    low_feat, low_place = pick(edge_index[0, 0, 0], edge_mask[0, 0, 0])
    high_feat, high_place = pick(edge_index[0, 0, 1], edge_mask[0, 0, 1])
    below_feat, below_place = passed_along((high_feat, high_place), "lat", 1)
    above_feat, above_place = passed_along((low_feat, low_place), "lat", -1)
    recv_feat = jnp.concatenate([below_feat, above_feat], 0)
    recv_place = jnp.concatenate([below_place, above_place], 0)
    cells = jnp.arange(height * width, dtype=jnp.int32)
    cell_rows = band_base + (cells // width).astype(jnp.float32)
    cell_cols = (cells % width).astype(jnp.float32)
    edge_weights = gauss_weights(
        cell_rows, cell_cols, recv_place[:, 0], recv_place[:, 1], recv_place[:, 2]
    )
    numer = jnp.dot(edge_weights, recv_feat, precision=lax.Precision.HIGHEST)
    denom = jnp.sum(edge_weights, 1)
    own_weights = gauss_weights(cell_rows, cell_cols, row_g, col_b, valid)
    numer = numer + jnp.dot(own_weights, feat, precision=lax.Precision.HIGHEST)
    denom = denom + jnp.sum(own_weights, 1)
    h0 = (
        (numer / jnp.sqrt(1.0 + denom)[:, None])
        .astype(jnp.bfloat16)
        .reshape(height, width, channels)
    )

    def fold_rows(patches, piece):
        return jnp.dot(patches, piece, preferred_element_type=jnp.float32)

    patches0 = padded_patches(haloed_rows(h0), height, width)
    pre1 = fold_rows(patches0, lax.all_gather(w_first, "dp", axis=0, tiled=True))
    h1 = jax.nn.silu(pre1).astype(jnp.bfloat16)
    patches1 = padded_patches(haloed_rows(h1.reshape(height, width, hidden)), height, width)
    pre2 = fold_rows(patches1, lax.all_gather(w_second, "dp", axis=0, tiled=True))
    encoded = (h1.astype(jnp.float32) + pre2).astype(jnp.bfloat16).reshape(1, height, width, hidden)
    cot = cotangent[0]
    cot_pad = haloed_rows(cot).reshape(-1, hidden)
    spread = lax.dot_general(
        cot_pad,
        lax.all_gather(w_second, "dp", axis=0, tiled=True),
        (((1,), (1,)), ((), ())),
        preferred_element_type=jnp.float32,
    )
    spread = spread.reshape(height + 2, width + 2, 9, hidden)
    dh1 = cot.astype(jnp.float32)
    for dy in range(3):
        for dx in range(3):
            dh1 = dh1 + spread[2 - dy : 2 - dy + height, 2 - dx : 2 - dx + width, dy * 3 + dx]
    sig = jax.nn.sigmoid(pre1)
    dpre1 = (dh1.reshape(-1, hidden) * sig * (1.0 + pre1 * (1.0 - sig))).astype(jnp.bfloat16)
    cot_flat = cot.reshape(-1, hidden)
    contract = (((0,), (0,)), ((), ()))
    grad_two = lax.dot_general(patches1, cot_flat, contract, preferred_element_type=jnp.float32)
    grad_one = lax.dot_general(patches0, dpre1, contract, preferred_element_type=jnp.float32)
    partial_one, partial_two = (
        lax.psum_scatter(
            grad_one.astype(jnp.bfloat16), "dp", scatter_dimension=0, tiled=True
        ).astype(jnp.float32),
        lax.psum_scatter(
            grad_two.astype(jnp.bfloat16), "dp", scatter_dimension=0, tiled=True
        ).astype(jnp.float32),
    )
    grad_first, grad_second = (
        lax.psum_scatter(
            partial_one.astype(jnp.bfloat16), "lat", scatter_dimension=1, tiled=True
        ).astype(jnp.float32),
        lax.psum_scatter(
            partial_two.astype(jnp.bfloat16), "lat", scatter_dimension=1, tiled=True
        ).astype(jnp.float32),
    )
    return (encoded, grad_first, grad_second)


def fits(mesh, height, width, hidden, channels, rows_one, rows_two):
    n_dp, n_lat = mesh.shape["dp"], mesh.shape["lat"]
    powers = all(n & (n - 1) == 0 for n in (n_dp, n_lat, hidden, channels))
    grid = height == 2 and width == channels and width % 128 == 0 and (height + 2) * channels == hidden
    blocks = all(
        [(d * rows + rows - 1) // size - d * rows // size for d in range(n_dp)] == [2] * n_dp
        for rows, size in ((rows_one, channels), (rows_two, hidden))
    )
    return powers and grid and n_dp == 2 * 2 and n_lat > 4 and (hidden // n_lat) % 32 == 0 and blocks and rows_one % 32 == 0 and rows_two % 128 == 0


def solution(mesh):
    in_specs = (
        P("dp", "lat", None),
        P("dp", "lat"),
        P("dp", "lat"),
        P("dp", "lat"),
        P("dp", "lat", None, None),
        P("dp", "lat", None, None),
        P("dp", "lat", None, None),
        P("dp", None),
        P("dp", None),
    )
    out_specs = (P("dp", "lat", None, None), P("dp", "lat"), P("dp", "lat"))

    def run(*args):
        feat, cot, w_first, w_second = args[0], args[6], args[7], args[8]
        n_dp, n_lat = mesh.shape["dp"], mesh.shape["lat"]
        shapes = (cot.shape[1] // n_lat, *cot.shape[2:], feat.shape[2], w_first.shape[0] // n_dp, w_second.shape[0] // n_dp)
        step = local if fits(mesh, *shapes) else plain
        return jax.shard_map(step, mesh=mesh, in_specs=in_specs, out_specs=out_specs, check_vma=False)(*args)

    return run
```

```python
import functools
import math

import jax
import jax.numpy as jnp
from jax import lax
from jax.experimental import pallas as pl
from jax.experimental.pallas import tpu as pltpu
from jax.sharding import PartitionSpec as P

BF16 = jnp.bfloat16
F32 = jnp.float32
VMEM = pl.BlockSpec(memory_space=pltpu.VMEM)
SMEM = pl.BlockSpec(memory_space=pltpu.SMEM)
FAR = pl.BlockSpec(memory_space=pltpu.HBM)


def call(kernel, name, outs, scratch=(), scalars=1, far=0, grant=48):
    def run(*args):
        return pl.pallas_call(
            kernel,
            name=name,
            out_shape=outs,
            in_specs=[SMEM] * scalars + [VMEM] * (len(args) - scalars - far) + [FAR] * far,
            out_specs=[VMEM] * len(outs),
            scratch_shapes=list(scratch),
            cost_estimate=pl.CostEstimate(flops=COST[name], bytes_accessed=0, transcendentals=0),
            compiler_params=pltpu.CompilerParams(vmem_limit_bytes=grant * 2**20),
        )(*args)

    return run


COST = {"edges": 4107269028, "own": 657163044, "finish": 1150035328, "back": 4600141312, "first": 24202651983, "turn": 2957233700, "gradsecond": 4107269028, "dpre": 1314326089, "gradfirst": 2464361417, "second": 4435850551, "add": 1150035328, "meet": 1150035328, "last": 1150035328}


def like(shape, dtype):
    return jax.ShapeDtypeStruct(shape, dtype)


def dot(a, b):
    return jnp.dot(a, b, preferred_element_type=F32)


def dot_nt(a, b):
    return lax.dot_general(a, b, (((1,), (1,)), ((), ())), preferred_element_type=F32)


def shifted(x, step, width):
    if isinstance(step, int) and step == 0:
        return x
    total = x.shape[0]
    wide = pltpu.roll(x.astype(F32), lax.rem(total - step, total) if not isinstance(step, int) else (total - step) % total, 0)
    place = lax.broadcasted_iota(jnp.int32, x.shape, 0) % width + step
    return jnp.where((place >= 0) & (place < width), wide, 0.0).astype(x.dtype)


def column_factor(col_ref, width):
    cells = lax.broadcasted_iota(jnp.int32, (width, col_ref.shape[1]), 0).astype(F32)
    away = cells - col_ref[...]
    return jnp.exp(-0.5 * (away * away))


def cell_weights(factor, row_ref, rows):
    parts = []
    for row in rows:
        away = row - row_ref[...]
        parts.append((factor * jnp.exp(-0.5 * (away * away))).astype(BF16))
    return jnp.concatenate(parts, axis=0)


def edge_kernel(height, width, s_ref, *refs):
    far, (first_ref, second_ref), near, sems = refs[:6], refs[6:8], refs[8:14], refs[14]
    copies = [pltpu.make_async_copy(a, b, sems.at[n]) for n, (a, b) in enumerate(zip(far, near))]
    for copy in copies:
        copy.start()
    for copy in copies[1:5]:
        copy.wait()
    feat_ref, row_ref, col_ref, index_ref, mask_ref, cot_ref = near
    up = lax.rem(lax.axis_index("lat"), 2) == 0
    slots, channels = feat_ref.shape
    factor = column_factor(col_ref, width)
    entries = index_ref.shape[1]
    slot = lax.broadcasted_iota(jnp.int32, (slots, entries), 0)
    live = slot < s_ref[0, 0]
    counted = []
    for side in range(2):
        named = jnp.where((slot == index_ref[side : side + 1]) & live, mask_ref[side : side + 1], 0)
        times = jnp.sum(named.astype(F32), axis=1, keepdims=True)
        offset = height if side == 1 else -height
        counted.append((times, cell_weights(factor, row_ref, [float(offset + i) for i in range(height)])))
    copies[0].wait()
    copies[5].wait()
    feat = feat_ref[...]
    totals = []
    for times, weights in counted:
        values = jnp.concatenate([feat * times, jnp.broadcast_to(times, feat.shape)], axis=1)
        totals.append(dot(weights, values.astype(BF16)))
    low, high = cot_ref[:width], cot_ref[(height - 1) * width :]
    lanes = feat_ref.shape[1]
    for out_ref, side in ((first_ref, jnp.where(up, high, low)), (second_ref, jnp.where(up, low, high))):
        for q in range(side.shape[1] // lanes):
            at = height * (width + 16) + q * width
            out_ref[at : at + width] = side[:, q * lanes : (q + 1) * lanes]
    for out_ref, one, other in ((first_ref, 1, 0), (second_ref, 0, 1)):
        total = jnp.where(up, totals[one], totals[other])
        out_ref[: height * width] = total[:, :channels].astype(BF16)
        for i in range(height):
            turned = total[i * width : (i + 1) * width, channels:].T[:16]
            out_ref[height * width + 16 * i : height * width + 16 * (i + 1)] = turned.astype(BF16)


def own_kernel(height, width, s_ref, feat_ref, row_ref, col_ref, numer_ref, denom_ref):
    slots, channels = feat_ref.shape
    live = lax.broadcasted_iota(jnp.int32, (slots, channels), 0) < s_ref[0, 0]
    values = jnp.concatenate([jnp.where(live, feat_ref[...], 0.0), live.astype(F32)], axis=1)
    weights = cell_weights(column_factor(col_ref, width), row_ref, [float(i) for i in range(height)])
    total = dot(weights, values.astype(BF16))
    numer_ref[...] = total[:, :channels]
    denom_ref[...] = total[:, channels:]


def partners(s_ref):
    first = jnp.where(s_ref[2] == 1, s_ref[4], s_ref[3])
    second = jnp.where(s_ref[2] == 1, s_ref[3], s_ref[4])
    return first, second


def finish_kernel(height, width, s_ref, numer_ref, denom_ref, first_ref, second_ref, out_ref, side_ref):
    first, second = partners(s_ref)
    cells = height * width

    def got(part):
        return jnp.where(first == 1, first_ref[part].astype(F32), 0.0) + jnp.where(
            second == 1, second_ref[part].astype(F32), 0.0
        )

    for i in range(height):
        rows = slice(i * width, (i + 1) * width)
        added = got(slice(cells + 16 * i, cells + 16 * i + 16))[:1]
        added = jnp.broadcast_to(added, (width, width)).T[:, : numer_ref.shape[1]]
        numer = numer_ref[rows] + got(rows)
        out_ref[rows] = (numer * lax.rsqrt(1.0 + denom_ref[rows] + added)).astype(BF16)
    lanes = numer_ref.shape[1]
    for n, ref in enumerate((first_ref, second_ref)):
        for q in range(side_ref.shape[1] // lanes):
            at = height * (width + 16) + q * width
            side_ref[n * width : (n + 1) * width, q * lanes : (q + 1) * lanes] = ref[at : at + width]


def side_rows(s_ref, first, second):
    up = s_ref[2] == 1
    none = jnp.zeros_like(first)
    below = jnp.where(s_ref[3] == 1, jnp.where(up, second, first), none)
    above = jnp.where(s_ref[4] == 1, jnp.where(up, first, second), none)
    return below, above


def first_kernel(height, width, offsets, s_ref, own_ref, a_ref, b_ref, w_near, w_far, *refs):
    pre_ref, h1_ref, edge_ref, near_ref, w_full = refs
    channels = own_ref.shape[1]
    count, piece, hidden = w_near.shape
    for place, offset in enumerate(offsets):
        at = lax.bitwise_xor(s_ref[5], offset) * piece
        w_full[pl.ds(pl.multiple_of(at, 32), piece)] = (w_near, w_far)[place // count][place % count]
    below, above = side_rows(s_ref, a_ref[...], b_ref[...])
    grid = jnp.concatenate([below[-2 * width :], own_ref[...], above[: 2 * width]], axis=0)
    rows = height + 2
    moved = [shifted(grid, step, width) for step in (-1, 0, 1)]
    patches = jnp.concatenate([moved[dx][dy * width : (dy + rows) * width] for dy in range(3) for dx in range(3)], axis=1)
    pre = dot(patches, w_full[...])
    h1 = (pre * jax.nn.sigmoid(pre)).astype(BF16)
    zero = jnp.zeros((width, hidden), BF16)
    pre_ref[...] = pre[width:-width]
    h1_ref[...] = h1[width:-width]
    edge_ref[:width] = jnp.where(s_ref[3] == 1, h1[:width], zero)
    edge_ref[width:] = jnp.where(s_ref[4] == 1, h1[-width:], zero)
    near = grid[width:-width]
    for i in range(rows):
        near_ref[:, i * channels : (i + 1) * channels] = near[i * width : (i + 1) * width]


def wide_rows(s_ref, width, cot_ref, side_ref):
    below, above = side_rows(s_ref, side_ref[:width], side_ref[width:])
    return jnp.concatenate([below, cot_ref[...], above], axis=0)


def chunk_place(s_ref, step, per_group, per_block):
    chunk = s_ref[6] * per_group + step
    block = chunk // per_block
    return block // 3, block % 3, chunk % per_block


def back_kernel(height, width, chunk, s_ref, cot_ref, cot_got, side_ref, side_got, w_ref, own_ref, other_ref, stack_ref, moved_ref):
    hidden = w_ref.shape[1]
    halves = hidden // chunk
    cells = height * width
    per_group = w_ref.shape[0] // chunk
    for place, ref in enumerate((cot_ref, cot_got, side_ref, side_got)):
        stack_ref[place] = ref[...]
    for member, out_ref in enumerate((own_ref, other_ref)):
        grid = wide_rows(s_ref, width, (cot_ref, cot_got)[member], (side_ref, side_got)[member])
        for dx in range(3):
            moved_ref[member, dx] = shifted(grid, 1 - dx, width)
        totals = [jnp.zeros((cells, chunk), F32) for _ in range(halves)]
        for step in range(per_group):
            dy, dx, _ = chunk_place(s_ref, step, per_group, halves)
            rows = pl.ds(pl.multiple_of((2 - dy) * width, width), cells)
            totals[step % halves] += dot_nt(moved_ref[member, dx, rows], w_ref[step * chunk : (step + 1) * chunk])
        start = chunk_place(s_ref, 0, per_group, halves)[2]
        for rank in range(halves):
            half = lax.rem(start + rank, halves)
            columns = pl.ds(pl.multiple_of(half * chunk, chunk), chunk)
            out_ref[:, columns] = totals[rank].astype(out_ref.dtype)


def second_kernel(height, width, chunk, s_ref, mid_one, mid_two, edge_one, edge_two, w_ref, own_ref, other_ref, moved_ref):
    hidden = w_ref.shape[1]
    halves = hidden // chunk
    cells = height * width
    per_group = w_ref.shape[0] // chunk
    for member, (mid_ref, edge_ref, out_ref) in enumerate(((mid_one, edge_one, own_ref), (mid_two, edge_two, other_ref))):
        grid = jnp.concatenate([edge_ref[:width], mid_ref[...], edge_ref[width:]], axis=0)
        for dx in range(3):
            place = shifted(grid, dx - 1, width)
            for half in range(halves):
                moved_ref[member, dx, half] = place[:, half * chunk : (half + 1) * chunk]
        total = mid_ref[...].astype(F32) if member == 0 else jnp.zeros((cells, hidden), F32)
        for step in range(per_group):
            dy, dx, half = chunk_place(s_ref, step, per_group, halves)
            rows = pl.ds(pl.multiple_of(dy * width, width), cells)
            total += dot(moved_ref[member, dx, half, rows], w_ref[step * chunk : (step + 1) * chunk])
        out_ref[...] = total.astype(out_ref.dtype)


def dpre_kernel(s_ref, pre_ref, cot_ref, near_ref, own_ref, got_ref, out_ref):
    pre = pre_ref[...]
    back = cot_ref[...].astype(F32) + own_ref[...] + got_ref[...].astype(F32)
    sig = jax.nn.sigmoid(pre)
    hidden, cells = pre.shape[1], pre.shape[0]
    out_ref[:hidden] = (back * sig * (1.0 + pre * (1.0 - sig))).T.astype(BF16)
    width = near_ref.shape[0]
    for half in range(near_ref.shape[1] // cells):
        out_ref[hidden + half * width : hidden + (half + 1) * width] = near_ref[:, half * cells : (half + 1) * cells]


def turn_kernel(height, width, rows_out, s_ref, *refs):
    near_ref, far_ref, out_ref, wide_ref = refs
    times, count = wide_ref.shape[0], wide_ref.shape[0] // 2
    _, cells, hidden = near_ref.shape
    first = (s_ref[5] * rows_out) // hidden
    for t in range(times):
        ref = (near_ref, far_ref)[t // count]
        wide_ref[t] = wide_rows(s_ref, width, ref.at[t % count], ref.at[count + t % count])
    for dx in range(3):
        j = lax.rem(dx + 3 - lax.rem(first, 3), 3)
        dy = jnp.minimum(first + j, 8) // 3
        rows = pl.ds(pl.multiple_of((2 - dy) * width, width), cells)
        for t in range(times):
            x = shifted(wide_ref[t, rows], 1 - dx, width)
            out_ref[j, :, t * cells : (t + 1) * cells] = x.astype(F32).T.astype(BF16)


def grad_second_kernel(rows_out, blocks, lats, s_ref, turned_ref, *refs):
    h1_refs, (keep_one, send_one, keep_two, send_two, full_ref) = refs[:-5], refs[-5:]
    hidden = h1_refs[0].shape[1]
    base = s_ref[5] * rows_out
    off = base - (base // hidden) * hidden
    h1 = jnp.concatenate([h1_ref[...] for h1_ref in h1_refs], axis=0)
    for j in range(blocks):
        full_ref[:, j * hidden : (j + 1) * hidden] = dot(turned_ref[j], h1)
    part = hidden // lats
    half = part // 2
    columns = pl.ds(pl.multiple_of(off, 128), rows_out)
    slots = [0] * 4
    for k in range(lats):
        at = lax.bitwise_xor(s_ref[0], k) * part
        for number, (keep_ref, send_ref, bit) in enumerate(((keep_one, send_one, 1), (keep_two, send_two, 2))):
            sent = 1 if k & bit else 0
            place = 2 * number + sent
            rows = pl.ds(pl.multiple_of(at + number * half, half), half)
            (keep_ref, send_ref)[sent][slots[place]] = full_ref[rows, columns].astype(BF16)
            slots[place] += 1


def grad_first_kernel(height, width, rows_out, lats, distance, s_ref, *refs):
    sent_refs, (keep_ref, send_ref, full_ref) = refs[:-3], refs[-3:]
    cells = sent_refs[0].shape[1]
    channels = full_ref.shape[2]
    rows = height + 2
    hidden = rows * channels
    wide = 3 * channels
    part = hidden // lats
    for t, sent_ref in enumerate(sent_refs):
        for i in range(rows):
            half, side = i // height, i % height
            full_ref[t, i * width : (i + 1) * width] = sent_ref[
                hidden + half * width : hidden + (half + 1) * width, side * channels : (side + 1) * channels
            ]
    for out_ref, away in ((send_ref, distance), (keep_ref, 0)):
        base = lax.bitwise_xor(s_ref[5], away) * rows_out
        first = base // channels
        off = base - first * channels
        turn = lax.rem(first, 3)
        total = jnp.zeros((hidden, wide), F32)
        for t, sent_ref in enumerate(sent_refs):
            pieces = []
            for dx in range(3):
                dy = jnp.minimum(first + lax.rem(dx + 3 - turn, 3), 8) // 3
                near = full_ref[t, pl.ds(pl.multiple_of(dy * width, width), cells)]
                pieces.append(shifted(near, dx - 1, width))
            total += dot(sent_ref[:hidden], jnp.concatenate(pieces, axis=1))
        total = pltpu.roll(total, lax.rem(2 * wide - off - turn * channels, wide), 1)[:, :rows_out].astype(BF16)
        for k in range(lats):
            out_ref[lax.bitwise_xor(s_ref[0], k)] = total[k * part : (k + 1) * part]


def add_kernel(places, *refs):
    count = len(places)
    for n, (stay, go) in enumerate(places):
        keep_ref, got_ref = refs[2 * n : 2 * n + 2]
        stay_ref, go_ref = refs[2 * (count + n) : 2 * (count + n) + 2]
        for out_ref, picked in ((stay_ref, stay), (go_ref, go)):
            for slot, place in enumerate(picked):
                out_ref[slot] = (keep_ref[place].astype(F32) + got_ref[place].astype(F32)).astype(BF16)


def meet_kernel(one_ref, got_one, two_ref, got_two, stay_ref, go_ref):
    half = one_ref.shape[1]
    for rows, keep_ref, got_ref in ((slice(0, half), one_ref, got_one), (slice(half, 2 * half), two_ref, got_two)):
        for place in range(keep_ref.shape[0]):
            out_ref = (stay_ref, go_ref)[place % 2]
            out_ref[place // 2, rows] = (keep_ref[place].astype(F32) + got_ref[place].astype(F32)).astype(BF16)


def last_kernel(keep_ref, got_ref, out_ref):
    out_ref[...] = keep_ref[0].astype(F32) + got_ref[0].astype(F32)


def swap(value, axis, bit):
    return lax.ppermute(value, axis, [(i, i ^ bit) for i in range(lax.axis_size(axis))])


def after(value, other):
    return lax.optimization_barrier((value, other))[0]


def distances(bits):
    order = [0]
    for bit in bits:
        order = order + [n ^ bit for n in order]
    return order


def with_partners(first, second):
    size = lax.axis_size("lat")
    pairs = [(i, i + 1) for i in range(1, size - 1, 2)]
    pairs = pairs + [(j, i) for i, j in pairs] + [(0, 0), (size - 1, size - 1)]
    return swap(first, "lat", 1), lax.ppermute(second, "lat", pairs)


def parted(offsets, bit):
    stay = [n for n, k in enumerate(offsets) if not k & bit]
    go = [n for n, k in enumerate(offsets) if k & bit]
    return (stay, go), [offsets[n] for n in stay]


def add_step(streams, offsets, bits):
    places, left = zip(*[parted(o, b) for o, b in zip(offsets, bits)])
    outs = [like((len(side), *keep.shape[1:]), BF16) for (keep, _), place in zip(streams, places) for side in place]
    flat = call(functools.partial(add_kernel, places), "add", outs, scalars=0)(*[v for pair in streams for v in pair])
    return [flat[n : n + 2] for n in range(0, len(flat), 2)], list(left)


def finished(stay, got, offsets, bits):
    for bit in bits:
        ((stay, go),), (offsets,) = add_step([(stay, got)], [offsets], [bit])
        got = swap(go, "lat", bit)
    return call(last_kernel, "last", [like(stay.shape[1:], F32)], scalars=0)(stay, got)[0].T


def local(obs_feat, obs_row, obs_col, counts, edge_index, edge_mask, cotangent, w_first, w_second):
    _, height, width, hidden = cotangent.shape
    channels = obs_feat.shape[2]
    cells = height * width
    n_dp, n_lat = lax.axis_size("dp"), lax.axis_size("lat")
    band, member = lax.axis_index("lat"), lax.axis_index("dp")
    scalars = jnp.stack(
        [
            band,
            counts[0, 0],
            1 - band % 2,
            (band > 0).astype(jnp.int32),
            (band < n_lat - 1).astype(jnp.int32),
            member,
            member // 2,
        ]
    ).astype(jnp.int32)
    lat_bits = [1 << n for n in range(n_lat.bit_length() - 1)]
    outer = n_dp // 2
    cot = cotangent[0].reshape(cells, hidden)

    feat, row, col = obs_feat[0], obs_row, obs_col
    payload = like((height * (width + 16) + width * hidden // channels, channels), BF16)
    observed = [feat, row, col, edge_index[0, 0], edge_mask[0, 0], cot]
    edges = call(
        functools.partial(edge_kernel, height, width),
        "edges",
        [payload, payload],
        scratch=[pltpu.VMEM(v.shape, v.dtype) for v in observed] + [pltpu.SemaphoreType.DMA((len(observed),))],
        far=len(observed),
        grant=60,
    )(counts, *observed)
    cot_got, w_got, w_other = swap(cot, "dp", outer), swap(w_first, "dp", outer), swap(w_second, "dp", 1)
    from_first, from_second = with_partners(*edges)
    numer, denom = call(functools.partial(own_kernel, height, width), "own", [like((cells, channels), F32)] * 2)(
        after(counts, w_other), feat, row, col
    )
    sides_out = like((2 * width, hidden), BF16)
    h0, side = call(functools.partial(finish_kernel, height, width), "finish", [like((cells, channels), BF16), sides_out])(
        scalars, numer, denom, from_first, from_second
    )
    h0_first, h0_second = with_partners(h0, h0)
    side_got = swap(side, "dp", outer)
    lower = member % 2 == 0
    w_two = jnp.concatenate([jnp.where(lower, w_second, w_other), jnp.where(lower, w_other, w_second)], axis=0)
    w_two = after(w_two, h0)
    chunk = math.gcd(w_two.shape[0], hidden)
    wide_cells = (height + 2) * width
    partial_outs = [like((cells, hidden), F32), like((cells, hidden), BF16)]
    back, back_other, stack = call(
        functools.partial(back_kernel, height, width, chunk),
        "back",
        partial_outs + [like((4, cells, hidden), BF16)],
        scratch=[pltpu.VMEM((2, 3, wide_cells, hidden), BF16)],
    )(after(scalars, h0), cot, cot_got, side, side_got, w_two)
    back_got = swap(back_other, "dp", outer)

    w_near = jnp.stack([w_first, after(w_got, h0)])
    w_far = swap(w_near, "dp", 1)
    pre1, h1, edge, h0_near = call(
        functools.partial(first_kernel, height, width, distances([outer, 1])),
        "first",
        [
            like((cells, hidden), F32),
            like((cells, hidden), BF16),
            sides_out,
            like((width, (height + 2) * channels), BF16),
        ],
        scratch=[pltpu.VMEM((n_dp * w_first.shape[0], hidden), BF16)],
    )(after(scalars, back), h0, h0_first, h0_second, w_near, w_far)

    h1_got = swap(h1, "dp", outer)
    h1_far, h1_far_got, stack_far = [swap(v, "dp", 1) for v in (h1, h1_got, stack)]

    rows_two, rows_one = w_second.shape[0], w_first.shape[0]
    part = hidden // n_lat
    turned = call(
        functools.partial(turn_kernel, height, width, rows_two),
        "turn",
        [like((3, hidden, n_dp * cells), BF16)],
        scratch=[pltpu.VMEM((n_dp, wide_cells, hidden), BF16)],
    )(after(scalars, (h1, back_got)), stack, stack_far)[0]
    piece = like((n_lat // 2, part // 2, rows_two), BF16)
    keep_one, send_one, keep_two, send_two = call(
        functools.partial(grad_second_kernel, rows_two, 3, n_lat),
        "gradsecond",
        [piece] * 4,
        scratch=[pltpu.VMEM((hidden, 3 * hidden), F32)],
    )(scalars, turned, h1, h1_got, h1_far, h1_far_got)
    sent = call(dpre_kernel, "dpre", [like((hidden + (height + 2) // height * width, cells), BF16)])(
        after(scalars, keep_one), pre1, cot, h0_near, back, back_got
    )[0]
    streams = [(keep_one, swap(send_one, "lat", 1)), (keep_two, swap(send_two, "lat", 2))]
    offsets = [[k for k in range(n_lat) if not k & bit] for bit in (1, 2)]
    ((stay_one, go_one), (stay_two, go_two)), _ = add_step(streams, offsets, (2, 1))
    got_one, got_two = swap(go_one, "lat", 2), swap(go_two, "lat", 1)
    stay, go = call(meet_kernel, "meet", [like((n_lat // 8, part, rows_two), BF16)] * 2, scalars=0)(
        stay_one, got_one, stay_two, got_two
    )
    grad_second = finished(stay, swap(go, "lat", 4), list(range(0, n_lat, 8)), lat_bits[3:])

    keep, send = call(
        functools.partial(grad_first_kernel, height, width, rows_one, n_lat, outer),
        "gradfirst",
        [like((n_lat, part, rows_one), BF16)] * 2,
        scratch=[pltpu.VMEM((2, wide_cells, channels), BF16)],
    )(scalars, sent, swap(sent, "dp", 1))
    first_got = swap(send, "dp", outer)
    grad_first = finished(after(keep, streams), first_got, list(range(n_lat)), lat_bits)

    edge_got = swap(after(edge, send), "dp", outer)
    second, second_other = call(
        functools.partial(second_kernel, height, width, chunk),
        "second",
        partial_outs,
        scratch=[pltpu.VMEM((2, 3, hidden // chunk, wide_cells, chunk), BF16)],
    )(after(scalars, first_got), h1, h1_got, edge, edge_got, w_two)
    encoded = (second + swap(second_other, "dp", outer).astype(F32)).astype(BF16).reshape(1, height, width, hidden)
    return encoded, grad_first, grad_second


def with_halo(value, sides, width):
    for axis, dim in sides:
        size, length = (lax.axis_size(axis), value.shape[dim])
        up = [(i, (i + 1) % size) for i in range(size - 1)]
        down = [(j, i) for i, j in up]
        last = lax.slice_in_dim(value, length - width, length, axis=dim)
        first = lax.slice_in_dim(value, 0, width, axis=dim)
        before = lax.ppermute(last, axis, up)
        after = lax.ppermute(first, axis, down)
        value = jnp.concatenate([before, value, after], axis=dim)
    return value


def passed_along(block, axis, distance):
    devices = range(lax.axis_size(axis))
    route = [(i - distance, i) for i in devices if i - distance in devices]
    return lax.ppermute(block, axis, route)


def gauss_weights(cell_rows, cell_cols, rows, cols, valid):
    drow = cell_rows[:, None] - rows[None, :]
    dcol = cell_cols[:, None] - cols[None, :]
    return valid[None, :] * jnp.exp(-0.5 * (drow * drow + dcol * dcol))


def haloed_rows(grid):
    padded = with_halo(grid, (("lat", 0),), 1)
    return jnp.pad(padded, ((0, 0), (1, 1), (0, 0)))


def padded_patches(padded, height, width):
    pieces = [padded[dy : dy + height, dx : dx + width] for dy in range(3) for dx in range(3)]
    return jnp.concatenate(pieces, axis=-1).reshape(height * width, -1)


def plain(obs_feat, obs_row, obs_col, counts, edge_index, edge_mask, cotangent, w_first, w_second):
    feat = obs_feat[0]
    slot_total = feat.shape[0]
    channels = feat.shape[1]
    height = cotangent.shape[1]
    width = cotangent.shape[2]
    hidden = cotangent.shape[3]
    band_index = lax.axis_index("lat")
    band_base = (band_index * height).astype(jnp.float32)
    count = counts[0, 0]
    row_g = obs_row[0] + band_base
    col_b = obs_col[0]
    slots = jnp.arange(slot_total, dtype=jnp.int32)
    valid = (slots < count).astype(jnp.float32)

    def pick(listed, listed_mask):
        picked_feat = jnp.take(feat, listed, axis=0)
        live_flag = listed_mask.astype(jnp.float32) * (listed < count).astype(jnp.float32)
        place = jnp.stack([jnp.take(row_g, listed), jnp.take(col_b, listed), live_flag], axis=1)
        return (picked_feat, place)

    low_feat, low_place = pick(edge_index[0, 0, 0], edge_mask[0, 0, 0])
    high_feat, high_place = pick(edge_index[0, 0, 1], edge_mask[0, 0, 1])
    below_feat, below_place = passed_along((high_feat, high_place), "lat", 1)
    above_feat, above_place = passed_along((low_feat, low_place), "lat", -1)
    recv_feat = jnp.concatenate([below_feat, above_feat], 0)
    recv_place = jnp.concatenate([below_place, above_place], 0)
    cells = jnp.arange(height * width, dtype=jnp.int32)
    cell_rows = band_base + (cells // width).astype(jnp.float32)
    cell_cols = (cells % width).astype(jnp.float32)
    edge_weights = gauss_weights(
        cell_rows, cell_cols, recv_place[:, 0], recv_place[:, 1], recv_place[:, 2]
    )
    numer = jnp.dot(edge_weights, recv_feat, precision=lax.Precision.HIGHEST)
    denom = jnp.sum(edge_weights, 1)
    own_weights = gauss_weights(cell_rows, cell_cols, row_g, col_b, valid)
    numer = numer + jnp.dot(own_weights, feat, precision=lax.Precision.HIGHEST)
    denom = denom + jnp.sum(own_weights, 1)
    h0 = (
        (numer / jnp.sqrt(1.0 + denom)[:, None])
        .astype(jnp.bfloat16)
        .reshape(height, width, channels)
    )

    def fold_rows(patches, piece):
        return jnp.dot(patches, piece, preferred_element_type=jnp.float32)

    patches0 = padded_patches(haloed_rows(h0), height, width)
    pre1 = fold_rows(patches0, lax.all_gather(w_first, "dp", axis=0, tiled=True))
    h1 = jax.nn.silu(pre1).astype(jnp.bfloat16)
    patches1 = padded_patches(haloed_rows(h1.reshape(height, width, hidden)), height, width)
    pre2 = fold_rows(patches1, lax.all_gather(w_second, "dp", axis=0, tiled=True))
    encoded = (h1.astype(jnp.float32) + pre2).astype(jnp.bfloat16).reshape(1, height, width, hidden)
    cot = cotangent[0]
    cot_pad = haloed_rows(cot).reshape(-1, hidden)
    spread = lax.dot_general(
        cot_pad,
        lax.all_gather(w_second, "dp", axis=0, tiled=True),
        (((1,), (1,)), ((), ())),
        preferred_element_type=jnp.float32,
    )
    spread = spread.reshape(height + 2, width + 2, 9, hidden)
    dh1 = cot.astype(jnp.float32)
    for dy in range(3):
        for dx in range(3):
            dh1 = dh1 + spread[2 - dy : 2 - dy + height, 2 - dx : 2 - dx + width, dy * 3 + dx]
    sig = jax.nn.sigmoid(pre1)
    dpre1 = (dh1.reshape(-1, hidden) * sig * (1.0 + pre1 * (1.0 - sig))).astype(jnp.bfloat16)
    cot_flat = cot.reshape(-1, hidden)
    contract = (((0,), (0,)), ((), ()))
    grad_two = lax.dot_general(patches1, cot_flat, contract, preferred_element_type=jnp.float32)
    grad_one = lax.dot_general(patches0, dpre1, contract, preferred_element_type=jnp.float32)
    partial_one, partial_two = (
        lax.psum_scatter(
            grad_one.astype(jnp.bfloat16), "dp", scatter_dimension=0, tiled=True
        ).astype(jnp.float32),
        lax.psum_scatter(
            grad_two.astype(jnp.bfloat16), "dp", scatter_dimension=0, tiled=True
        ).astype(jnp.float32),
    )
    grad_first, grad_second = (
        lax.psum_scatter(
            partial_one.astype(jnp.bfloat16), "lat", scatter_dimension=1, tiled=True
        ).astype(jnp.float32),
        lax.psum_scatter(
            partial_two.astype(jnp.bfloat16), "lat", scatter_dimension=1, tiled=True
        ).astype(jnp.float32),
    )
    return (encoded, grad_first, grad_second)


def fits(mesh, height, width, hidden, channels, rows_one, rows_two):
    n_dp, n_lat = mesh.shape["dp"], mesh.shape["lat"]
    powers = all(n & (n - 1) == 0 for n in (n_dp, n_lat, hidden, channels))
    grid = height == 2 and width == channels and width % 128 == 0 and (height + 2) * channels == hidden
    blocks = all(
        [(d * rows + rows - 1) // size - d * rows // size for d in range(n_dp)] == [2] * n_dp
        for rows, size in ((rows_one, channels), (rows_two, hidden))
    )
    return powers and grid and n_dp == 2 * 2 and n_lat > 4 and (hidden // n_lat) % 32 == 0 and blocks and rows_one % 32 == 0 and rows_two % 128 == 0


def solution(mesh):
    in_specs = (
        P("dp", "lat", None),
        P("dp", "lat"),
        P("dp", "lat"),
        P("dp", "lat"),
        P("dp", "lat", None, None),
        P("dp", "lat", None, None),
        P("dp", "lat", None, None),
        P("dp", None),
        P("dp", None),
    )
    out_specs = (P("dp", "lat", None, None), P("dp", "lat"), P("dp", "lat"))

    def run(*args):
        feat, cot, w_first, w_second = args[0], args[6], args[7], args[8]
        n_dp, n_lat = mesh.shape["dp"], mesh.shape["lat"]
        shapes = (cot.shape[1] // n_lat, *cot.shape[2:], feat.shape[2], w_first.shape[0] // n_dp, w_second.shape[0] // n_dp)
        step = local if fits(mesh, *shapes) else plain
        return jax.shard_map(step, mesh=mesh, in_specs=in_specs, out_specs=out_specs, check_vma=False)(*args)

    return run
```
